512 devices in a mesh: dp: 16 (over y, core), cell: 32 (over z, x).
Axes of the slice: x: 4, y: 8, z: 8, core: 2. Of those that a mesh axis runs over, the one named last changes fastest.
Arguments:
- blocks: bfloat16 [16, 32, 8, 256, 256], P('dp', 'cell'), may hold values from -0.375 to 0.375
- row_block: int32 [16, 32, 8], P('dp', 'cell'), may hold values from 0 to 5, as said below
- col_block: int32 [16, 32, 8], P('dp', 'cell'), may hold values from 0 to 5
- counts: int32 [16, 32], P('dp', 'cell'), may hold values from 2 to 8, as said below
- observed: float32 [24576, 128], P(('dp', 'cell'))
Outputs:
- model: float32 [49152, 128], P(('cell', 'dp'))
- residual: float32 [24576, 128], P(('dp', 'cell'))
The draws below stay inside these ranges and needn't reach their ends.
Inputs may be any that keep to these rules, and one draw needn't show every extreme that they name: Within one tile the slots name distinct positions (row_block, col_block); slots at or beyond the tile's count are ignored. `counts`: some tile has all 8 slots in use.
All inputs are finite; a program needn't handle non-finite values.
Results may differ from the reference program's by a relative error of at most 0.0057.
Values may be sent and summed in bfloat16 or wider, within the bound.
A program may use at most 64 MiB of HBM per device.

```python
import jax
import jax.numpy as jnp
from jax import lax

BS = 256
RB = 6
CB = 6
NBMAX = 8
K = 128
ITERS = 2
ND = 24576
NC = 49152
N_DP = 16
N_CELL = 32


def block_pattern(key):
    keys = jax.random.split(key, N_DP * N_CELL)
    flat = jax.vmap(lambda one: jax.random.permutation(one, RB * CB)[:NBMAX])(keys)
    return flat.reshape(N_DP, N_CELL, NBMAX).astype(jnp.int32)


def draw_row_block(key, part):
    pattern = block_pattern(key)
    return (pattern // CB).astype(jnp.int32)


def draw_col_block(key, part):
    pattern = block_pattern(key)
    return (pattern % CB).astype(jnp.int32)


def draw_counts(key, part):
    key = jax.random.fold_in(key, 5)
    first, second, third = jax.random.split(key, 3)
    lower = jax.random.randint(first, (N_DP * N_CELL,), 0, NBMAX + 1)
    upper = jax.random.randint(second, (N_DP * N_CELL,), 0, NBMAX + 1)
    loads = jnp.maximum(jnp.minimum(lower, upper), 2)
    chosen = jax.random.randint(third, (), 0, N_DP * N_CELL)
    loads = jnp.where(jnp.arange(N_DP * N_CELL) == chosen, NBMAX, loads)
    return loads.reshape(N_DP, N_CELL).astype(jnp.int32)


def draw_observed(key, part):
    key = jax.random.fold_in(key, 7)
    first, second, third = jax.random.split(key, 3)
    trend = 3.0 ** (jnp.arange(ND, dtype=jnp.float32) / ND)
    row_scale = 10.0 ** jax.random.uniform(second, (ND, 1), jnp.float32) * trend[:, None]
    col_scale = 10.0 ** jax.random.uniform(third, (1, K), jnp.float32)
    values = jax.random.normal(first, (ND, K), jnp.float32) * row_scale * col_scale * 0.3
    return values.astype(jnp.float32)


def level_of(key, shape, cuts, least, high):
    def one(axis_at, blocks):
        steps = jax.random.uniform(jax.random.fold_in(jax.random.fold_in(key, 6), axis_at), (blocks,), jnp.float32, least / len(cuts), high / len(cuts))
        return jnp.repeat(jnp.exp(steps), shape[axis_at] // blocks).reshape((-1,) + (1,) * (len(shape) - axis_at - 1))

    factor_of = one(*cuts[0])
    for cut in cuts[1:]:
        factor_of = factor_of * one(*cut)
    return factor_of


def bell_draw(key, dims, scale, bound, cuts=(), kind=jnp.bfloat16):
    array = jax.random.normal(key, dims, jnp.float32) * scale
    if len(cuts) > 0:
        array = level_of(key, dims, cuts, -0.22, 0.18) * array
    return jnp.clip(array, min=-bound, max=bound).astype(kind)


def setup_inputs(seed: int = 0) -> dict:
    splits = jax.random.split(jax.random.key(seed), 6)
    return {
        "blocks": bell_draw(splits[0], (N_DP, N_CELL, NBMAX, BS, BS), BS ** -0.5, 0.375, ((0, 16), (1, 32))),
        "row_block": draw_row_block(jax.random.fold_in(splits[5], 71), 0),
        "col_block": draw_col_block(jax.random.fold_in(splits[5], 71), 0),
        "counts": draw_counts(jax.random.fold_in(splits[5], 71), 0),
        "observed": draw_observed(jax.random.fold_in(splits[5], 71), 0),
    }


def tile_forward(tiles, rows, cols, count, vec):
    mask = (jnp.arange(NBMAX) < count).astype(jnp.float32)
    seg = vec.reshape(CB, BS, K)[cols].astype(jnp.float32)
    prod = jnp.einsum('bij,bjk->bik', tiles.astype(jnp.float32), seg) * mask[:, None, None]
    out = jnp.zeros((RB, BS, K), jnp.float32).at[rows].add(prod)
    return out.reshape(RB * BS, K)


def tile_adjoint(tiles, rows, cols, count, vec):
    mask = (jnp.arange(NBMAX) < count).astype(jnp.float32)
    seg = vec.reshape(RB, BS, K)[rows].astype(jnp.float32)
    prod = jnp.einsum('bji,bjk->bik', tiles.astype(jnp.float32), seg) * mask[:, None, None]
    out = jnp.zeros((CB, BS, K), jnp.float32).at[cols].add(prod)
    return out.reshape(CB * BS, K)


def apply_forward(blocks, row_block, col_block, counts, vec):
    pieces = vec.astype(jnp.bfloat16).reshape(N_CELL, CB * BS, K)

    def one_tile(index):
        i = index // N_CELL
        j = index % N_CELL
        return tile_forward(blocks[i, j], row_block[i, j], col_block[i, j], counts[i, j], pieces[j])

    parts = lax.map(one_tile, jnp.arange(N_DP * N_CELL, dtype=jnp.int32))
    return jnp.sum(parts.reshape(N_DP, N_CELL, RB * BS, K), axis=1).reshape(ND, K)


def apply_adjoint(blocks, row_block, col_block, counts, vec):
    pieces = vec.astype(jnp.bfloat16).reshape(N_DP, RB * BS, K)

    def one_tile(index):
        i = index // N_CELL
        j = index % N_CELL
        return tile_adjoint(blocks[i, j], row_block[i, j], col_block[i, j], counts[i, j], pieces[i])

    parts = lax.map(one_tile, jnp.arange(N_DP * N_CELL, dtype=jnp.int32))
    return jnp.sum(parts.reshape(N_DP, N_CELL, CB * BS, K), axis=0).reshape(NC, K)


def reference(blocks, row_block, col_block, counts, observed):
    residual = observed
    model = jnp.zeros((NC, K), jnp.float32)
    gradient = apply_adjoint(blocks, row_block, col_block, counts, residual)
    direction = gradient
    gamma = jnp.sum(gradient * gradient, axis=0)
    for step in range(ITERS):
        image = apply_forward(blocks, row_block, col_block, counts, direction)
        delta = jnp.sum(image * image, axis=0)
        alpha = gamma / delta
        model = model + alpha * direction
        residual = residual - alpha * image
        if step + 1 < ITERS:
            gradient = apply_adjoint(blocks, row_block, col_block, counts, residual)
            gamma_new = jnp.sum(gradient * gradient, axis=0)
            direction = gradient + (gamma_new / gamma) * direction
            gamma = gamma_new
    return model, residual
```

```python
import jax
import jax.numpy as jnp
from jax import lax
from jax.experimental import pallas as pl
from jax.experimental.pallas import tpu as pltpu
from jax.sharding import PartitionSpec as P

F32 = jnp.float32
BF16 = jnp.bfloat16
MESH = pl.DeviceIdType.MESH
SLOTS = 8
BLOCK = 256
NY = 8
NZ = 8
NX = 4
N_DP = NY * 2
N_CELL = NZ * NX
TILE = 6 * BLOCK
DROWS = TILE // N_CELL
CROWS = TILE // N_DP
COLS = 128


def far_first(i, n):
    return jnp.where(i % 2 == 1, n // 2 - (i + 1) // 2, n // 2 + i // 2)


def rows_at(ref, index, size):
    return ref.at[pl.ds(pl.multiple_of(index * size, size), size)]


def cgls(
    tiles,
    row_of,
    col_of,
    counts,
    observed,
    model_out,
    residual_out,
    tiles_t,
    pieces,
    prod,
    residual_full,
    image_full,
    direction_full,
    grad_send,
    pair_recv,
    grad_pair,
    grad_recv,
    image_send,
    image_recv,
    gamma_part,
    gamma_recv,
    delta_part,
    delta_recv,
    delta_dp_part,
    delta_cell,
    last_dp_part,
    last_dp,
    last_cell_part,
    last_cell,
    gather_send_sem,
    gather_recv_sem,
    dir_send_sem,
    dir_recv_sem,
    fwd_send_sem,
    fwd_recv_sem,
    pair_send_sem,
    pair_recv_sem,
    grad_send_sem,
    grad_recv_sem,
    image_send_sem,
    image_recv_sem,
    small_send_sem,
    small_recv_sem,
):
    dp = lax.axis_index("dp")
    cell = lax.axis_index("cell")
    y, core = dp // 2, dp % 2
    z, x = cell // NX, cell % NX
    sibling = (y * 2 + 1 - core, cell)

    def cell_peer(i):
        dz = far_first(i // NX, NZ)
        dx = far_first(i % NX, NX)
        return ((z + dz) % NZ) * NX + (x + dx) % NX

    def y_peer(i):
        return (y + far_first(i, NY)) % NY

    def dp_peer(i):
        return y_peer(i // 2) * 2 + (core + 1 + i) % 2

    def over_cells(step):
        lax.fori_loop(0, N_CELL - 1, lambda i, c: (step(cell_peer(i)), c)[1], 0)

    def over_dp(step):
        lax.fori_loop(0, N_DP - 1, lambda i, c: (step(dp_peer(i)), c)[1], 0)

    def over_y(step):
        lax.fori_loop(0, NY - 1, lambda i, c: (step(y_peer(i)), c)[1], 0)

    def remote(src, dst, send, recv, device):
        return pltpu.make_async_remote_copy(
            src_ref=src, dst_ref=dst, send_sem=send, recv_sem=recv, device_id=device, device_id_type=MESH
        )

    def wait_bytes(ref, sem):
        pltpu.make_async_copy(ref, ref, sem).wait()

    barrier = pltpu.get_barrier_semaphore()
    over_cells(lambda p: pl.semaphore_signal(barrier, inc=1, device_id=(dp, p), device_id_type=MESH))
    over_dp(lambda p: pl.semaphore_signal(barrier, inc=1, device_id=(p, cell), device_id_type=MESH))
    pl.semaphore_wait(barrier, N_CELL + N_DP - 2)

    used = counts[0, 0]

    def apply(matrix, source, target, vector, send):
        def multiply(slot, carry):
            prod[slot] = jnp.dot(matrix[slot], pieces[source[0, 0, slot]], preferred_element_type=F32)
            return carry

        for at in range(6):
            pieces[at] = vector[pl.ds(at * BLOCK, BLOCK), :]
        lax.fori_loop(0, SLOTS, multiply, 0)

        def place(at, carry):
            total = jnp.zeros((BLOCK, COLS), F32)
            for slot in range(SLOTS):
                here = jnp.logical_and(target[0, 0, slot] == at, slot < used)
                total = total + here.astype(F32) * prod[slot]
            send[pl.ds(pl.multiple_of(at * BLOCK, BLOCK), BLOCK), :] = total.astype(send.dtype)
            return carry

        lax.fori_loop(0, 6, place, 0)

    def gather_cells(full, k):
        mine = rows_at(full, cell, DROWS)
        over_cells(lambda p: remote(mine, mine, gather_send_sem.at[k], gather_recv_sem.at[k], (dp, p)).start())

    def gather_cells_wait(full, k):
        others = full.at[pl.ds(0, (N_CELL - 1) * DROWS)]
        wait_bytes(others, gather_recv_sem.at[k])
        wait_bytes(others, gather_send_sem.at[k])

    def gather_dp(full, k):
        mine = rows_at(full, dp, CROWS)
        over_y(lambda p: remote(mine, mine, dir_send_sem.at[k], dir_recv_sem.at[k, y], (p * 2 + core, cell)).start())
        remote(mine, mine, fwd_send_sem.at[k], fwd_recv_sem.at[k], sibling).start()

        def forward(i, carry):
            src = y_peer(NY - 2 - i)
            slot = rows_at(full, src * 2 + core, CROWS)
            wait_bytes(slot, dir_recv_sem.at[k, src])
            remote(slot, slot, fwd_send_sem.at[k], fwd_recv_sem.at[k], sibling).start()
            return carry

        lax.fori_loop(0, NY - 1, forward, 0)
        wait_bytes(full.at[pl.ds(0, NY * CROWS)], fwd_recv_sem.at[k])
        wait_bytes(full.at[pl.ds(0, NY * CROWS)], fwd_send_sem.at[k])
        wait_bytes(full.at[pl.ds(0, (NY - 1) * CROWS)], dir_send_sem.at[k])

    def scatter_dp(k):
        def pair(i, carry):
            src = rows_at(grad_send.at[k], i * 2 + 1 - core, CROWS)
            remote(src, rows_at(pair_recv.at[k], i, CROWS), pair_send_sem.at[k], pair_recv_sem.at[k], sibling).start()
            return carry

        lax.fori_loop(0, NY, pair, 0)
        wait_bytes(pair_recv.at[k], pair_recv_sem.at[k])

        def add(i, carry):
            at = far_first(i, NY)
            at = (y + at) % NY
            kept = grad_send[k, pl.ds(pl.multiple_of((at * 2 + core) * CROWS, CROWS), CROWS), :]
            got = pair_recv[k, pl.ds(pl.multiple_of(at * CROWS, CROWS), CROWS), :]
            grad_pair[k, pl.ds(pl.multiple_of(at * CROWS, CROWS), CROWS), :] = (kept + got).astype(BF16)
            return carry

        lax.fori_loop(0, NY, add, 0)
        slot = rows_at(grad_recv.at[k], y, CROWS)
        over_y(
            lambda p: remote(
                rows_at(grad_pair.at[k], p, CROWS), slot, grad_send_sem.at[k], grad_recv_sem.at[k], (p * 2 + core, cell)
            ).start()
        )
        grad_recv[k, pl.ds(pl.multiple_of(y * CROWS, CROWS), CROWS), :] = grad_pair[
            k, pl.ds(pl.multiple_of(y * CROWS, CROWS), CROWS), :
        ]

    def scatter_dp_wait(k):
        others = grad_recv.at[k, pl.ds(0, (NY - 1) * CROWS)]
        wait_bytes(others, grad_recv_sem.at[k])
        wait_bytes(others, grad_send_sem.at[k])
        wait_bytes(pair_recv.at[k], pair_send_sem.at[k])
        total = jnp.zeros((CROWS, COLS), F32)
        for i in range(NY):
            total = total + grad_recv[k, pl.ds(i * CROWS, CROWS), :].astype(F32)
        return total

    def scatter_cells(k):
        slot = rows_at(image_recv.at[k], cell, DROWS)

        def send(p):
            remote(
                rows_at(image_send.at[k], p, DROWS), slot, image_send_sem.at[k], image_recv_sem.at[k], (dp, p)
            ).start()

        over_cells(send)
        mine = pl.ds(pl.multiple_of(cell * DROWS, DROWS), DROWS)
        image_recv[k, mine, :] = image_send[k, mine, :]

    def scatter_cells_wait(k):
        others = image_recv.at[k, pl.ds(0, (N_CELL - 1) * DROWS)]
        wait_bytes(others, image_recv_sem.at[k])
        wait_bytes(others, image_send_sem.at[k])

        def add(i, total):
            return total + image_recv[k, pl.ds(pl.multiple_of(i * DROWS, DROWS), DROWS), :].astype(F32)

        return lax.fori_loop(0, N_CELL, add, jnp.zeros((DROWS, COLS), F32))

    def squares(full):
        def add(i, total):
            part = full[pl.ds(pl.multiple_of(i * 128, 128), 128), :].astype(F32)
            return total + part * part

        return jnp.sum(lax.fori_loop(0, TILE // 128, add, jnp.zeros((128, COLS), F32)), axis=0, keepdims=True)

    def small_over_cells(part, recv, k):
        recv[cell] = part[...]
        over_cells(
            lambda p: remote(part, recv.at[cell], small_send_sem.at[k], small_recv_sem.at[k], (dp, p)).start()
        )

    def small_over_dp(part, recv, k):
        recv[dp] = part[...]
        over_dp(lambda p: remote(part, recv.at[dp], small_send_sem.at[k], small_recv_sem.at[k], (p, cell)).start())

    def small_wait(recv, k, n):
        wait_bytes(recv.at[pl.ds(0, n - 1)], small_recv_sem.at[k])
        wait_bytes(recv.at[pl.ds(0, n - 1)], small_send_sem.at[k])
        return jnp.sum(recv[...], axis=0)

    residual_full[pl.ds(pl.multiple_of(cell * DROWS, DROWS), DROWS), :] = observed[...].astype(BF16)
    gather_cells(residual_full, 0)
    for slot in range(SLOTS):
        tiles_t[slot] = tiles[slot].T
    gather_cells_wait(residual_full, 0)

    apply(tiles_t, row_of, col_of, residual_full, grad_send.at[0])
    scatter_dp(0)
    gradient = scatter_dp_wait(0)
    model_out[...] = gradient
    my_cells = pl.ds(pl.multiple_of(dp * CROWS, CROWS), CROWS)
    my_rows = pl.ds(pl.multiple_of(cell * DROWS, DROWS), DROWS)

    direction_full[0, my_cells, :] = gradient.astype(BF16)
    gather_dp(direction_full.at[0], 0)
    apply(tiles, col_of, row_of, direction_full.at[0], image_send.at[0])
    scatter_cells(0)
    gamma_part[0] = squares(direction_full.at[0])
    small_over_cells(gamma_part.at[0], gamma_recv.at[0], 0)
    image = scatter_cells_wait(0)
    residual_out[...] = image
    gamma = small_wait(gamma_recv.at[0], 0, N_CELL)

    delta_part[...] = jnp.sum(image * image, axis=0, keepdims=True)
    small_over_dp(delta_part, delta_recv, 1)
    delta_dp_part[...] = small_wait(delta_recv, 1, N_DP)
    small_over_cells(delta_dp_part, delta_cell, 5)
    alpha = gamma / small_wait(delta_cell, 5, N_CELL)
    residual = observed[...] - alpha * image

    image_full[my_rows, :] = residual.astype(BF16)
    gather_cells(image_full, 1)
    gather_cells_wait(image_full, 1)
    apply(tiles_t, row_of, col_of, image_full, grad_send.at[1])
    scatter_dp(1)
    gradient = scatter_dp_wait(1)
    first = model_out[...]

    direction_full[1, my_cells, :] = gradient.astype(BF16)
    gather_dp(direction_full.at[1], 1)
    apply(tiles, col_of, row_of, direction_full.at[1], image_send.at[1])
    scatter_cells(1)
    gamma_part[1] = squares(direction_full.at[1])
    small_over_cells(gamma_part.at[1], gamma_recv.at[1], 2)
    image_one = scatter_cells_wait(1)
    gamma_one = small_wait(gamma_recv.at[1], 2, N_CELL)
    beta = gamma_one / gamma
    image_zero = residual_out[...]
    image_one = image_one + beta * image_zero

    last_dp_part[...] = jnp.sum(image_one * image_one, axis=0, keepdims=True)
    small_over_dp(last_dp_part, last_dp, 3)
    direction = gradient + beta * first
    model = alpha * first
    last_cell_part[...] = small_wait(last_dp, 3, N_DP)
    small_over_cells(last_cell_part, last_cell, 4)
    delta_one = small_wait(last_cell, 4, N_CELL)
    alpha_one = gamma_one / delta_one
    model_out[...] = model + alpha_one * direction
    residual_out[...] = residual - alpha_one * image_one


def shards(blocks, row_block, col_block, counts, observed):
    vmem = pl.BlockSpec(memory_space=pltpu.VMEM)
    smem = pl.BlockSpec(memory_space=pltpu.SMEM)
    dma = pltpu.SemaphoreType.DMA
    return pl.pallas_call(
        cgls,
        out_shape=(
            jax.ShapeDtypeStruct((CROWS, COLS), F32),
            jax.ShapeDtypeStruct((DROWS, COLS), F32),
        ),
        in_specs=[vmem, smem, smem, smem, vmem],
        out_specs=(vmem, vmem),
        scratch_shapes=[
            pltpu.VMEM((SLOTS, BLOCK, BLOCK), BF16),
            pltpu.VMEM((6, BLOCK, COLS), BF16),
            pltpu.VMEM((SLOTS, BLOCK, COLS), F32),
            pltpu.VMEM((TILE, COLS), BF16),
            pltpu.VMEM((TILE, COLS), BF16),
            pltpu.VMEM((2, TILE, COLS), BF16),
            pltpu.VMEM((2, TILE, COLS), F32),
            pltpu.VMEM((2, TILE // 2, COLS), F32),
            pltpu.VMEM((2, TILE // 2, COLS), BF16),
            pltpu.VMEM((2, TILE // 2, COLS), BF16),
            pltpu.VMEM((2, TILE, COLS), BF16),
            pltpu.VMEM((2, TILE, COLS), BF16),
            pltpu.VMEM((2, 1, COLS), F32),
            pltpu.VMEM((2, N_CELL, 1, COLS), F32),
            pltpu.VMEM((1, COLS), F32),
            pltpu.VMEM((N_DP, 1, COLS), F32),
            pltpu.VMEM((1, COLS), F32),
            pltpu.VMEM((N_CELL, 1, COLS), F32),
            pltpu.VMEM((1, COLS), F32),
            pltpu.VMEM((N_DP, 1, COLS), F32),
            pltpu.VMEM((1, COLS), F32),
            pltpu.VMEM((N_CELL, 1, COLS), F32),
            dma((2,)),
            dma((2,)),
            dma((2,)),
            dma((2, NY)),
            dma((2,)),
            dma((2,)),
            dma((2,)),
            dma((2,)),
            dma((2,)),
            dma((2,)),
            dma((2,)),
            dma((2,)),
            dma((6,)),
            dma((6,)),
        ],
        compiler_params=pltpu.CompilerParams(
            collective_id=0, has_side_effects=True, vmem_limit_bytes=40 * 1024 * 1024
        ),
        name="cgls",
    )(blocks[0, 0], row_block, col_block, counts, observed)


def solution(mesh):
    in_specs = (
        P("dp", "cell", None, None, None),
        P("dp", "cell", None),
        P("dp", "cell", None),
        P("dp", "cell"),
        P(("dp", "cell"), None),
    )
    out_specs = (P(("cell", "dp"), None), P(("dp", "cell"), None))
    return jax.shard_map(shards, mesh=mesh, in_specs=in_specs, out_specs=out_specs, check_vma=False)
```

```python
import jax
import jax.numpy as jnp
from jax import lax
from jax.experimental import pallas as pl
from jax.experimental.pallas import tpu as pltpu
from jax.sharding import PartitionSpec as P

F32 = jnp.float32
BF16 = jnp.bfloat16
MESH = pl.DeviceIdType.MESH
SLOTS = 8
BLOCK = 256
NY = 8
NZ = 8
NX = 4
N_DP = NY * 2
N_CELL = NZ * NX
TILE = 6 * BLOCK
DROWS = TILE // N_CELL
CROWS = TILE // N_DP
COLS = 128


def far_first(i, n):
    return n // 2 - (i + 1) // 2 if i % 2 == 1 else (n // 2 + i // 2) % n


def rows_at(ref, index, size):
    return ref.at[pl.ds(pl.multiple_of(index * size, size), size)]


def cgls(
    tiles_hbm,
    row_of,
    col_of,
    counts,
    observed,
    model_out,
    residual_out,
    tiles,
    tiles_t,
    pieces,
    prod,
    residual_full,
    direction_full,
    grad_send,
    pair_recv,
    grad_pair,
    grad_recv,
    image_send,
    image_recv,
    sums_mine,
    sums_dp,
    sums_mid,
    sums_cell,
    load_sem,
    gather_send_sem,
    gather_recv_sem,
    dir_send_sem,
    dir_recv_sem,
    fwd_send_sem,
    fwd_recv_sem,
    pair_send_sem,
    pair_recv_sem,
    grad_send_sem,
    grad_recv_sem,
    image_send_sem,
    image_recv_sem,
    small_send_sem,
    small_recv_sem,
):
    dp = lax.axis_index("dp")
    cell = lax.axis_index("cell")
    y, core = dp // 2, dp % 2
    z, x = cell // NX, cell % NX
    sibling = (y * 2 + 1 - core, cell)
    my_cells = pl.ds(pl.multiple_of(dp * CROWS, CROWS), CROWS)
    my_rows = pl.ds(pl.multiple_of(cell * DROWS, DROWS), DROWS)

    load = pltpu.make_async_copy(tiles_hbm, tiles, load_sem)
    load.start()

    def z_at(i):
        return (z + far_first(i, NZ)) % NZ

    def y_at(i):
        return (y + far_first(i, NY)) % NY

    def over_cells(step):
        for i in range(N_CELL - 1):
            step(z_at(i // NX) * NX + (x + far_first(i % NX, NX)) % NX, i // NX)

    def over_dp(step):
        for i in range(N_DP - 1):
            step(y_at(i // 2) * 2 + (core + 1 + i) % 2)

    def remote(src, dst, send, recv, device):
        return pltpu.make_async_remote_copy(
            src_ref=src, dst_ref=dst, send_sem=send, recv_sem=recv, device_id=device, device_id_type=MESH
        )

    def wait_bytes(ref, sem):
        pltpu.make_async_copy(ref, ref, sem).wait()

    barrier = pltpu.get_barrier_semaphore()
    over_cells(lambda p, _: pl.semaphore_signal(barrier, inc=1, device_id=(dp, p), device_id_type=MESH))
    over_dp(lambda p: pl.semaphore_signal(barrier, inc=1, device_id=(p, cell), device_id_type=MESH))
    residual_full[0, my_rows, :] = observed[...].astype(BF16)
    load.wait()
    for slot in range(SLOTS):
        tiles_t[slot] = tiles[slot].T
    pl.semaphore_wait(barrier, N_CELL + N_DP - 2)

    used = counts[0, 0]

    def apply(matrix, source, target, vector, send):
        for at in range(6):
            pieces[at] = vector[pl.ds(at * BLOCK, BLOCK), :]
        for slot in range(SLOTS):
            prod[slot] = jnp.dot(matrix[slot], pieces[source[0, 0, slot]], preferred_element_type=F32)

        def place(at, carry):
            total = jnp.zeros((BLOCK, COLS), F32)
            for slot in range(SLOTS):
                here = jnp.logical_and(target[0, 0, slot] == at, slot < used)
                total = total + here.astype(F32) * prod[slot]
            send[pl.ds(pl.multiple_of(at * BLOCK, BLOCK), BLOCK), :] = total.astype(send.dtype)
            return carry

        lax.fori_loop(0, 6, place, 0)

    def gather_cells(k):
        mine = residual_full.at[k, my_rows]
        over_cells(lambda p, _: remote(mine, mine, gather_send_sem.at[k], gather_recv_sem.at[k], (dp, p)).start())
        others = residual_full.at[k, pl.ds(0, (N_CELL - 1) * DROWS)]
        wait_bytes(others, gather_recv_sem.at[k])
        wait_bytes(others, gather_send_sem.at[k])

    def gather_dp(k):
        full = direction_full.at[k]
        mine = full.at[my_cells]
        for i in range(NY - 1):
            remote(mine, mine, dir_send_sem.at[k], dir_recv_sem.at[k, y], (y_at(i) * 2 + core, cell)).start()
        remote(mine, mine, fwd_send_sem.at[k], fwd_recv_sem.at[k], sibling).start()
        for i in range(NY - 1):
            src = y_at(NY - 2 - i)
            slot = rows_at(full, src * 2 + core, CROWS)
            wait_bytes(slot, dir_recv_sem.at[k, src])
            remote(slot, slot, fwd_send_sem.at[k], fwd_recv_sem.at[k], sibling).start()
        wait_bytes(full.at[pl.ds(0, NY * CROWS)], fwd_recv_sem.at[k])
        wait_bytes(full.at[pl.ds(0, NY * CROWS)], fwd_send_sem.at[k])
        wait_bytes(full.at[pl.ds(0, (NY - 1) * CROWS)], dir_send_sem.at[k])

    def scatter_dp(k):
        for i in range(NY):
            at = y_at(i)
            src = rows_at(grad_send.at[k], at * 2 + 1 - core, CROWS)
            remote(src, rows_at(pair_recv.at[k], at, CROWS), pair_send_sem.at[k], pair_recv_sem.at[k, at], sibling).start()
        slot = rows_at(grad_recv.at[k], y, CROWS)
        for i in range(NY):
            at = y_at(i)
            rows = pl.ds(pl.multiple_of(at * CROWS, CROWS), CROWS)
            wait_bytes(pair_recv.at[k, rows], pair_recv_sem.at[k, at])
            both = grad_send[k, pl.ds(pl.multiple_of((at * 2 + core) * CROWS, CROWS), CROWS), :] + pair_recv[k, rows, :]
            if i < NY - 1:
                grad_pair[k, rows, :] = both.astype(BF16)
                remote(
                    grad_pair.at[k, rows], slot, grad_send_sem.at[k], grad_recv_sem.at[k, y], (at * 2 + core, cell)
                ).start()
            else:
                total = both
        for i in range(NY - 1):
            src = y_at(NY - 2 - i)
            rows = pl.ds(pl.multiple_of(src * CROWS, CROWS), CROWS)
            wait_bytes(grad_recv.at[k, rows], grad_recv_sem.at[k, src])
            total = total + grad_recv[k, rows, :].astype(F32)
        wait_bytes(grad_recv.at[k, pl.ds(0, (NY - 1) * CROWS)], grad_send_sem.at[k])
        wait_bytes(pair_recv.at[k], pair_send_sem.at[k])
        return total

    def scatter_cells(k):
        slot = image_recv.at[k, my_rows]

        def send(p, group):
            remote(
                rows_at(image_send.at[k], p, DROWS), slot, image_send_sem.at[k], image_recv_sem.at[k, z], (dp, p)
            ).start()

        over_cells(send)
        image_recv[k, my_rows, :] = image_send[k, my_rows, :]
        total = jnp.zeros((DROWS, COLS), F32)
        for i in range(NZ):
            src = z_at(NZ - 1 - i)
            start = pl.multiple_of(src * NX * DROWS, NX * DROWS)
            count = NX - 1 if i == 0 else NX
            wait_bytes(image_recv.at[k, pl.ds(start, count * DROWS)], image_recv_sem.at[k, src])
            for j in range(NX):
                total = total + image_recv[k, pl.ds(start + j * DROWS, DROWS), :].astype(F32)
        wait_bytes(image_recv.at[k, pl.ds(0, (N_CELL - 1) * DROWS)], image_send_sem.at[k])
        return total

    def column(values):
        return jnp.sum(values, axis=0, keepdims=True)

    def sum_all(k, rows):
        sums_mine[k] = jnp.zeros((8, COLS), F32)
        for i, row in enumerate(rows):
            sums_mine[k, pl.ds(i, 1), :] = row
        mine = sums_mine.at[k]
        over_dp(
            lambda p: remote(mine, sums_dp.at[k, dp], small_send_sem.at[k, 0], small_recv_sem.at[k, 0], (p, cell)).start()
        )
        sums_dp[k, dp] = sums_mine[k]
        wait_bytes(sums_dp.at[k, pl.ds(0, N_DP - 1)], small_recv_sem.at[k, 0])
        sums_mid[k] = jnp.sum(sums_dp[k], axis=0)
        half = sums_mid.at[k]
        over_cells(
            lambda p, _: remote(
                half, sums_cell.at[k, cell], small_send_sem.at[k, 1], small_recv_sem.at[k, 1], (dp, p)
            ).start()
        )
        sums_cell[k, cell] = sums_mid[k]
        wait_bytes(sums_cell.at[k, pl.ds(0, N_CELL - 1)], small_recv_sem.at[k, 1])
        total = jnp.sum(sums_cell[k], axis=0)
        wait_bytes(sums_dp.at[k, pl.ds(0, N_DP - 1)], small_send_sem.at[k, 0])
        wait_bytes(sums_cell.at[k, pl.ds(0, N_CELL - 1)], small_send_sem.at[k, 1])
        return [total[i : i + 1] for i in range(len(rows))]

    gather_cells(0)
    apply(tiles_t, row_of, col_of, residual_full.at[0], grad_send.at[0])
    gradient = scatter_dp(0)
    model_out[...] = gradient

    direction_full[0, my_cells, :] = gradient.astype(BF16)
    gather_dp(0)
    apply(tiles, col_of, row_of, direction_full.at[0], image_send.at[0])
    image = scatter_cells(0)

    first = model_out[...]
    gamma, delta = sum_all(0, [column(first * first), column(image * image)])
    alpha = gamma / delta
    residual = observed[...] - alpha * image
    residual_out[...] = image

    residual_full[1, my_rows, :] = residual.astype(BF16)
    gather_cells(1)
    apply(tiles_t, row_of, col_of, residual_full.at[1], grad_send.at[1])
    gradient = scatter_dp(1)

    direction_full[1, my_cells, :] = gradient.astype(BF16)
    gather_dp(1)
    apply(tiles, col_of, row_of, direction_full.at[1], image_send.at[1])
    update = scatter_cells(1)
    image = residual_out[...]
    gamma_one, update_square, cross = sum_all(
        1, [column(gradient * gradient), column(update * update), column(update * image)]
    )
    beta = gamma_one / gamma
    delta_one = update_square + beta * (2.0 * cross + beta * delta)
    alpha_one = gamma_one / delta_one
    first = model_out[...]
    model_out[...] = alpha * first + alpha_one * (gradient + beta * first)
    residual_out[...] = observed[...] - alpha * image - alpha_one * (update + beta * image)


def shards(blocks, row_block, col_block, counts, observed):
    vmem = pl.BlockSpec(memory_space=pltpu.VMEM)
    smem = pl.BlockSpec(memory_space=pltpu.SMEM)
    dma = pltpu.SemaphoreType.DMA
    return pl.pallas_call(
        cgls,
        out_shape=(
            jax.ShapeDtypeStruct((CROWS, COLS), F32),
            jax.ShapeDtypeStruct((DROWS, COLS), F32),
        ),
        in_specs=[pl.BlockSpec(memory_space=pl.ANY), smem, smem, smem, vmem],
        out_specs=(vmem, vmem),
        scratch_shapes=[
            pltpu.VMEM((SLOTS, BLOCK, BLOCK), BF16),
            pltpu.VMEM((SLOTS, BLOCK, BLOCK), BF16),
            pltpu.VMEM((6, BLOCK, COLS), BF16),
            pltpu.VMEM((SLOTS, BLOCK, COLS), F32),
            pltpu.VMEM((2, TILE, COLS), BF16),
            pltpu.VMEM((2, TILE, COLS), BF16),
            pltpu.VMEM((2, TILE, COLS), F32),
            pltpu.VMEM((2, TILE // 2, COLS), F32),
            pltpu.VMEM((2, TILE // 2, COLS), BF16),
            pltpu.VMEM((2, TILE // 2, COLS), BF16),
            pltpu.VMEM((2, TILE, COLS), BF16),
            pltpu.VMEM((2, TILE, COLS), BF16),
            pltpu.VMEM((2, 8, COLS), F32),
            pltpu.VMEM((2, N_DP, 8, COLS), F32),
            pltpu.VMEM((2, 8, COLS), F32),
            pltpu.VMEM((2, N_CELL, 8, COLS), F32),
            dma,
            dma((2,)),
            dma((2,)),
            dma((2,)),
            dma((2, NY)),
            dma((2,)),
            dma((2,)),
            dma((2,)),
            dma((2, NY)),
            dma((2,)),
            dma((2, NY)),
            dma((2,)),
            dma((2, NZ)),
            dma((2, 2)),
            dma((2, 2)),
        ],
        compiler_params=pltpu.CompilerParams(
            collective_id=0, has_side_effects=True, vmem_limit_bytes=40 * 1024 * 1024
        ),
        name="cgls",
    )(blocks[0, 0], row_block, col_block, counts, observed)


def solution(mesh):
    in_specs = (
        P("dp", "cell", None, None, None),
        P("dp", "cell", None),
        P("dp", "cell", None),
        P("dp", "cell"),
        P(("dp", "cell"), None),
    )
    out_specs = (P(("cell", "dp"), None), P(("dp", "cell"), None))
    return jax.shard_map(shards, mesh=mesh, in_specs=in_specs, out_specs=out_specs, check_vma=False)
```

```python
import jax
import jax.numpy as jnp
from jax import lax
from jax.experimental import pallas as pl
from jax.experimental.pallas import tpu as pltpu
from jax.sharding import PartitionSpec as P

F32 = jnp.float32
BF16 = jnp.bfloat16
MESH = pl.DeviceIdType.MESH
SLOTS = 8
BLOCK = 256
NY = 8
NZ = 8
NX = 4
N_DP = NY * 2
N_CELL = NZ * NX
TILE = 6 * BLOCK
DROWS = TILE // N_CELL
CROWS = TILE // N_DP
COLS = 128


def far_first(i, n):
    return n // 2 - (i + 1) // 2 if i % 2 == 1 else (n // 2 + i // 2) % n


def rows_of(index, size):
    return pl.ds(pl.multiple_of(index * size, size), size)


def rows_at(ref, index, size):
    return ref.at[rows_of(index, size)]


def cgls(
    tiles_hbm,
    row_of,
    col_of,
    counts,
    observed,
    model_out,
    residual_out,
    tiles,
    tiles_t,
    pieces,
    prod,
    residual_full,
    direction_full,
    grad_send,
    pair_recv,
    grad_pair,
    grad_recv,
    image_send,
    line_recv,
    image_line,
    image_recv,
    sums_mine,
    sums_dp,
    sums_mid,
    sums_cell,
    load_sem,
    gather_send_sem,
    gather_z_sem,
    gather_x_sem,
    dir_send_sem,
    dir_recv_sem,
    fwd_send_sem,
    fwd_recv_sem,
    pair_send_sem,
    pair_recv_sem,
    grad_send_sem,
    grad_recv_sem,
    line_send_sem,
    line_recv_sem,
    image_send_sem,
    image_recv_sem,
    small_send_sem,
    small_recv_sem,
):
    dp = lax.axis_index("dp")
    cell = lax.axis_index("cell")
    y, core = dp // 2, dp % 2
    z, x = cell // NX, cell % NX
    sibling = (y * 2 + 1 - core, cell)
    my_cells = pl.ds(pl.multiple_of(dp * CROWS, CROWS), CROWS)
    my_rows = pl.ds(pl.multiple_of(cell * DROWS, DROWS), DROWS)

    load = pltpu.make_async_copy(tiles_hbm, tiles, load_sem)
    load.start()

    def z_at(i):
        return (z + far_first(i, NZ)) % NZ

    def x_at(i):
        return (x + far_first(i, NX)) % NX

    def y_at(i):
        return (y + far_first(i, NY)) % NY

    def over_cells(step):
        for i in range(N_CELL - 1):
            step(z_at(i // NX) * NX + x_at(i % NX))

    def over_dp(step):
        for i in range(N_DP - 1):
            step(y_at(i // 2) * 2 + (core + 1 + i) % 2)

    def remote(src, dst, send, recv, device):
        return pltpu.make_async_remote_copy(
            src_ref=src, dst_ref=dst, send_sem=send, recv_sem=recv, device_id=device, device_id_type=MESH
        )

    def wait_bytes(ref, sem):
        pltpu.make_async_copy(ref, ref, sem).wait()

    barrier = pltpu.get_barrier_semaphore()
    greet = [(dp, z_at(i) * NX + x) for i in range(NZ - 1)] + [(y_at(i) * 2 + core, cell) for i in range(NY - 1)]
    greet += [(dp, z * NX + x_at(i)) for i in range(NX - 1)] + [sibling]
    for device in greet:
        pl.semaphore_signal(barrier, inc=1, device_id=device, device_id_type=MESH)
    residual_full[0, my_rows, :] = observed[...].astype(BF16)
    load.wait()
    for slot in range(SLOTS):
        tiles_t[slot] = tiles[slot].T
    pl.semaphore_wait(barrier, len(greet))

    used = counts[0, 0]

    def apply(matrix, source, target, vector, send):
        for at in range(6):
            pieces[at] = vector[pl.ds(at * BLOCK, BLOCK), :]
        for slot in range(SLOTS):
            prod[slot] = jnp.dot(matrix[slot], pieces[source[0, 0, slot]], preferred_element_type=F32)

        def place(at, carry):
            total = jnp.zeros((BLOCK, COLS), F32)
            for slot in range(SLOTS):
                here = jnp.logical_and(target[0, 0, slot] == at, slot < used)
                total = total + here.astype(F32) * prod[slot]
            send[pl.ds(pl.multiple_of(at * BLOCK, BLOCK), BLOCK), :] = total.astype(send.dtype)
            return carry

        lax.fori_loop(0, 6, place, 0)

    def gather_cells(k):
        full = residual_full.at[k]
        mine = full.at[my_rows]
        for i in range(NZ - 1):
            remote(mine, mine, gather_send_sem.at[k], gather_z_sem.at[k, z], (dp, z_at(i) * NX + x)).start()
        for i in range(NX - 1):
            remote(mine, mine, gather_send_sem.at[k], gather_x_sem.at[k], (dp, z * NX + x_at(i))).start()
        for i in range(NZ - 1):
            src = z_at(NZ - 2 - i)
            slot = rows_at(full, src * NX + x, DROWS)
            wait_bytes(slot, gather_z_sem.at[k, src])
            for j in range(NX - 1):
                remote(slot, slot, gather_send_sem.at[k], gather_x_sem.at[k], (dp, z * NX + x_at(j))).start()
        wait_bytes(full.at[pl.ds(0, NZ * (NX - 1) * DROWS)], gather_x_sem.at[k])
        wait_bytes(full.at[pl.ds(0, (N_CELL - 1) * DROWS)], gather_send_sem.at[k])

    def gather_dp(k):
        full = direction_full.at[k]
        mine = full.at[my_cells]
        for i in range(NY - 1):
            remote(mine, mine, dir_send_sem.at[k], dir_recv_sem.at[k, y], (y_at(i) * 2 + core, cell)).start()
        remote(mine, mine, fwd_send_sem.at[k], fwd_recv_sem.at[k], sibling).start()
        for i in range(NY - 1):
            src = y_at(NY - 2 - i)
            slot = rows_at(full, src * 2 + core, CROWS)
            wait_bytes(slot, dir_recv_sem.at[k, src])
            remote(slot, slot, fwd_send_sem.at[k], fwd_recv_sem.at[k], sibling).start()
        wait_bytes(full.at[pl.ds(0, NY * CROWS)], fwd_recv_sem.at[k])
        wait_bytes(full.at[pl.ds(0, NY * CROWS)], fwd_send_sem.at[k])
        wait_bytes(full.at[pl.ds(0, (NY - 1) * CROWS)], dir_send_sem.at[k])

    def scatter_dp(k):
        for i in range(NY):
            at = y_at(i)
            src = rows_at(grad_send.at[k], at * 2 + 1 - core, CROWS)
            remote(src, rows_at(pair_recv.at[k], at, CROWS), pair_send_sem.at[k], pair_recv_sem.at[k, at], sibling).start()
        slot = rows_at(grad_recv.at[k], y, CROWS)
        for i in range(NY):
            at = y_at(i)
            rows = pl.ds(pl.multiple_of(at * CROWS, CROWS), CROWS)
            wait_bytes(pair_recv.at[k, rows], pair_recv_sem.at[k, at])
            both = grad_send[k, pl.ds(pl.multiple_of((at * 2 + core) * CROWS, CROWS), CROWS), :] + pair_recv[k, rows, :]
            if i < NY - 1:
                grad_pair[k, rows, :] = both.astype(BF16)
                remote(
                    grad_pair.at[k, rows], slot, grad_send_sem.at[k], grad_recv_sem.at[k, y], (at * 2 + core, cell)
                ).start()
            else:
                total = both
        for i in range(NY - 1):
            src = y_at(NY - 2 - i)
            rows = pl.ds(pl.multiple_of(src * CROWS, CROWS), CROWS)
            wait_bytes(grad_recv.at[k, rows], grad_recv_sem.at[k, src])
            total = total + grad_recv[k, rows, :].astype(F32)
        wait_bytes(grad_recv.at[k, pl.ds(0, (NY - 1) * CROWS)], grad_send_sem.at[k])
        wait_bytes(pair_recv.at[k], pair_send_sem.at[k])
        return total

    def scatter_cells(k):
        for i in range(NZ):
            to = z_at(i)
            slot = rows_at(line_recv.at[k], to * NX + x, DROWS)
            for j in range(NX - 1):
                src = rows_at(image_send.at[k], to * NX + x_at(j), DROWS)
                remote(src, slot, line_send_sem.at[k], line_recv_sem.at[k, to], (dp, z * NX + x_at(j))).start()
        for i in range(NZ):
            to = z_at(i)
            wait_bytes(line_recv.at[k, pl.ds(0, (NX - 1) * DROWS)], line_recv_sem.at[k, to])
            total = image_send[k, rows_of(to * NX + x, DROWS), :].astype(F32)
            for j in range(NX - 1):
                total = total + line_recv[k, rows_of(to * NX + x_at(j), DROWS), :].astype(F32)
            if i < NZ - 1:
                image_line[k, rows_of(to, DROWS), :] = total
                remote(
                    rows_at(image_line.at[k], to, DROWS),
                    rows_at(image_recv.at[k], z, DROWS),
                    image_send_sem.at[k],
                    image_recv_sem.at[k, z],
                    (dp, to * NX + x),
                ).start()
        for i in range(NZ - 1):
            src = z_at(NZ - 2 - i)
            wait_bytes(rows_at(image_recv.at[k], src, DROWS), image_recv_sem.at[k, src])
            total = total + image_recv[k, rows_of(src, DROWS), :]
        wait_bytes(line_recv.at[k, pl.ds(0, NZ * (NX - 1) * DROWS)], line_send_sem.at[k])
        wait_bytes(image_recv.at[k, pl.ds(0, (NZ - 1) * DROWS)], image_send_sem.at[k])
        return total

    def column(values):
        return jnp.sum(values, axis=0, keepdims=True)

    def sum_all(k, rows):
        sums_mine[k] = jnp.zeros((8, COLS), F32)
        for i, row in enumerate(rows):
            sums_mine[k, pl.ds(i, 1), :] = row
        mine = sums_mine.at[k]
        over_dp(
            lambda p: remote(mine, sums_dp.at[k, dp], small_send_sem.at[k, 0], small_recv_sem.at[k, 0], (p, cell)).start()
        )
        sums_dp[k, dp] = sums_mine[k]
        wait_bytes(sums_dp.at[k, pl.ds(0, N_DP - 1)], small_recv_sem.at[k, 0])
        sums_mid[k] = jnp.sum(sums_dp[k], axis=0)
        half = sums_mid.at[k]
        over_cells(
            lambda p: remote(
                half, sums_cell.at[k, cell], small_send_sem.at[k, 1], small_recv_sem.at[k, 1], (dp, p)
            ).start()
        )
        sums_cell[k, cell] = sums_mid[k]
        wait_bytes(sums_cell.at[k, pl.ds(0, N_CELL - 1)], small_recv_sem.at[k, 1])
        total = jnp.sum(sums_cell[k], axis=0)
        wait_bytes(sums_dp.at[k, pl.ds(0, N_DP - 1)], small_send_sem.at[k, 0])
        wait_bytes(sums_cell.at[k, pl.ds(0, N_CELL - 1)], small_send_sem.at[k, 1])
        return [total[i : i + 1] for i in range(len(rows))]

    gather_cells(0)
    apply(tiles_t, row_of, col_of, residual_full.at[0], grad_send.at[0])
    gradient = scatter_dp(0)
    model_out[...] = gradient

    direction_full[0, my_cells, :] = gradient.astype(BF16)
    gather_dp(0)
    apply(tiles, col_of, row_of, direction_full.at[0], image_send.at[0])
    image = scatter_cells(0)

    first = model_out[...]
    gamma, delta = sum_all(0, [column(first * first), column(image * image)])
    alpha = gamma / delta
    residual = observed[...] - alpha * image
    residual_out[...] = image

    residual_full[1, my_rows, :] = residual.astype(BF16)
    gather_cells(1)
    apply(tiles_t, row_of, col_of, residual_full.at[1], grad_send.at[1])
    gradient = scatter_dp(1)

    direction_full[1, my_cells, :] = gradient.astype(BF16)
    gather_dp(1)
    apply(tiles, col_of, row_of, direction_full.at[1], image_send.at[1])
    update = scatter_cells(1)
    image = residual_out[...]
    gamma_one, update_square, cross = sum_all(
        1, [column(gradient * gradient), column(update * update), column(update * image)]
    )
    beta = gamma_one / gamma
    delta_one = update_square + beta * (2.0 * cross + beta * delta)
    alpha_one = gamma_one / delta_one
    first = model_out[...]
    model_out[...] = alpha * first + alpha_one * (gradient + beta * first)
    residual_out[...] = observed[...] - alpha * image - alpha_one * (update + beta * image)


def shards(blocks, row_block, col_block, counts, observed):
    vmem = pl.BlockSpec(memory_space=pltpu.VMEM)
    smem = pl.BlockSpec(memory_space=pltpu.SMEM)
    dma = pltpu.SemaphoreType.DMA
    return pl.pallas_call(
        cgls,
        out_shape=(
            jax.ShapeDtypeStruct((CROWS, COLS), F32),
            jax.ShapeDtypeStruct((DROWS, COLS), F32),
        ),
        in_specs=[pl.BlockSpec(memory_space=pl.ANY), smem, smem, smem, vmem],
        out_specs=(vmem, vmem),
        scratch_shapes=[
            pltpu.VMEM((SLOTS, BLOCK, BLOCK), BF16),
            pltpu.VMEM((SLOTS, BLOCK, BLOCK), BF16),
            pltpu.VMEM((6, BLOCK, COLS), BF16),
            pltpu.VMEM((SLOTS, BLOCK, COLS), F32),
            pltpu.VMEM((2, TILE, COLS), BF16),
            pltpu.VMEM((2, TILE, COLS), BF16),
            pltpu.VMEM((2, TILE, COLS), F32),
            pltpu.VMEM((2, TILE // 2, COLS), F32),
            pltpu.VMEM((2, TILE // 2, COLS), BF16),
            pltpu.VMEM((2, TILE // 2, COLS), BF16),
            pltpu.VMEM((2, TILE, COLS), BF16),
            pltpu.VMEM((2, TILE, COLS), BF16),
            pltpu.VMEM((2, NZ * DROWS, COLS), F32),
            pltpu.VMEM((2, NZ * DROWS, COLS), F32),
            pltpu.VMEM((2, 8, COLS), F32),
            pltpu.VMEM((2, N_DP, 8, COLS), F32),
            pltpu.VMEM((2, 8, COLS), F32),
            pltpu.VMEM((2, N_CELL, 8, COLS), F32),
            dma,
            dma((2,)),
            dma((2, NZ)),
            dma((2,)),
            dma((2,)),
            dma((2, NY)),
            dma((2,)),
            dma((2,)),
            dma((2,)),
            dma((2, NY)),
            dma((2,)),
            dma((2, NY)),
            dma((2,)),
            dma((2, NZ)),
            dma((2,)),
            dma((2, NZ)),
            dma((2, 2)),
            dma((2, 2)),
        ],
        compiler_params=pltpu.CompilerParams(
            collective_id=0, has_side_effects=True, vmem_limit_bytes=60 * 1024 * 1024
        ),
        name="cgls",
    )(blocks[0, 0], row_block, col_block, counts, observed)


def solution(mesh):
    in_specs = (
        P("dp", "cell", None, None, None),
        P("dp", "cell", None),
        P("dp", "cell", None),
        P("dp", "cell"),
        P(("dp", "cell"), None),
    )
    out_specs = (P(("cell", "dp"), None), P(("dp", "cell"), None))
    return jax.shard_map(shards, mesh=mesh, in_specs=in_specs, out_specs=out_specs, check_vma=False)
```

```python
import jax
import jax.numpy as jnp
from jax import lax
from jax.experimental import pallas as pl
from jax.experimental.pallas import tpu as pltpu
from jax.sharding import PartitionSpec as P

F32 = jnp.float32
BF16 = jnp.bfloat16
MESH = pl.DeviceIdType.MESH
SLOTS = 8
BLOCK = 256
NY = 8
NZ = 8
NX = 4
N_DP = NY * 2
N_CELL = NZ * NX
TILE = 6 * BLOCK
DROWS = TILE // N_CELL
CROWS = TILE // N_DP
COLS = 128
TINY = 1e-30


def far_first(i, n):
    return n // 2 - (i + 1) // 2 if i % 2 == 1 else (n // 2 + i // 2) % n


def rows_of(index, size):
    return pl.ds(pl.multiple_of(index * size, size), size)


def rows_at(ref, index, size):
    return ref.at[rows_of(index, size)]


def cgls(
    tiles_hbm,
    row_of,
    col_of,
    counts,
    observed,
    model_out,
    residual_out,
    tiles,
    tiles_t,
    pieces,
    wide_pieces,
    prod,
    image_exact,
    residual_full,
    direction_full,
    grad_send,
    pair_recv,
    grad_pair,
    grad_recv,
    image_send,
    line_recv,
    image_line,
    image_recv,
    sums_mine,
    sums_dp,
    sums_mid,
    sums_cell,
    load_sem,
    gather_send_sem,
    gather_z_sem,
    gather_x_sem,
    dir_send_sem,
    dir_recv_sem,
    fwd_send_sem,
    fwd_recv_sem,
    pair_send_sem,
    pair_recv_sem,
    grad_send_sem,
    grad_recv_sem,
    line_send_sem,
    line_recv_sem,
    image_send_sem,
    image_recv_sem,
    small_send_sem,
    small_recv_sem,
):
    dp = lax.axis_index("dp")
    cell = lax.axis_index("cell")
    y, core = dp // 2, dp % 2
    z, x = cell // NX, cell % NX
    sibling = (y * 2 + 1 - core, cell)
    my_cells = pl.ds(pl.multiple_of(dp * CROWS, CROWS), CROWS)
    my_rows = pl.ds(pl.multiple_of(cell * DROWS, DROWS), DROWS)

    load = pltpu.make_async_copy(tiles_hbm, tiles, load_sem)
    load.start()

    def z_at(i):
        return (z + far_first(i, NZ)) % NZ

    def x_at(i):
        return (x + far_first(i, NX)) % NX

    def y_at(i):
        return (y + far_first(i, NY)) % NY

    def over_cells(step):
        for i in range(N_CELL - 1):
            step(z_at(i // NX) * NX + x_at(i % NX))

    def over_dp(step):
        for i in range(N_DP - 1):
            step(y_at(i // 2) * 2 + (core + 1 + i) % 2)

    def remote(src, dst, send, recv, device):
        return pltpu.make_async_remote_copy(
            src_ref=src, dst_ref=dst, send_sem=send, recv_sem=recv, device_id=device, device_id_type=MESH
        )

    def wait_bytes(ref, sem):
        pltpu.make_async_copy(ref, ref, sem).wait()

    barrier = pltpu.get_barrier_semaphore()
    greet = [(dp, z_at(i) * NX + x) for i in range(NZ - 1)] + [(y_at(i) * 2 + core, cell) for i in range(NY - 1)]
    greet += [(dp, z * NX + x_at(i)) for i in range(NX - 1)] + [sibling]
    for device in greet:
        pl.semaphore_signal(barrier, inc=1, device_id=device, device_id_type=MESH)
    residual_full[0, my_rows, :] = observed[...].astype(BF16)
    load.wait()
    for slot in range(SLOTS):
        tiles_t[slot] = tiles[slot].T
    pl.semaphore_wait(barrier, len(greet))

    used = counts[0, 0]

    def multiply(matrix, source):
        for slot in range(SLOTS):
            prod[slot] = jnp.dot(matrix[slot], pieces[source[0, 0, slot]], preferred_element_type=F32)

    def apply(matrix, source, target, vector, sends):
        for at in range(6):
            pieces[at] = vector[pl.ds(at * BLOCK, BLOCK), :]
        multiply(matrix, source)
        place(target, sends)

    def place(target, sends):
        def one(at, carry):
            total = jnp.zeros((BLOCK, COLS), F32)
            for slot in range(SLOTS):
                here = jnp.logical_and(target[0, 0, slot] == at, slot < used)
                total = total + here.astype(F32) * prod[slot]
            for send in sends:
                send[rows_of(at, BLOCK), :] = total.astype(send.dtype)
            return carry

        lax.fori_loop(0, 6, one, 0)

    def gather_cells(k, between=None):
        full = residual_full.at[k]
        mine = full.at[my_rows]
        for i in range(NZ - 1):
            remote(mine, mine, gather_send_sem.at[k], gather_z_sem.at[k, z], (dp, z_at(i) * NX + x)).start()
        for i in range(NX - 1):
            remote(mine, mine, gather_send_sem.at[k], gather_x_sem.at[k], (dp, z * NX + x_at(i))).start()
        for i in range(NZ - 1):
            if i == 4 and between is not None:
                between()
            src = z_at(NZ - 2 - i)
            slot = rows_at(full, src * NX + x, DROWS)
            wait_bytes(slot, gather_z_sem.at[k, src])
            for j in range(NX - 1):
                remote(slot, slot, gather_send_sem.at[k], gather_x_sem.at[k], (dp, z * NX + x_at(j))).start()
        wait_bytes(full.at[pl.ds(0, NZ * (NX - 1) * DROWS)], gather_x_sem.at[k])
        wait_bytes(full.at[pl.ds(0, (N_CELL - 1) * DROWS)], gather_send_sem.at[k])

    def gather_dp(k):
        full = direction_full.at[k]
        mine = full.at[my_cells]
        for i in range(NY - 1):
            remote(mine, mine, dir_send_sem.at[k], dir_recv_sem.at[k, y], (y_at(i) * 2 + core, cell)).start()
        remote(mine, mine, fwd_send_sem.at[k], fwd_recv_sem.at[k], sibling).start()
        for i in range(NY - 1):
            src = y_at(NY - 2 - i)
            slot = rows_at(full, src * 2 + core, CROWS)
            wait_bytes(slot, dir_recv_sem.at[k, src])
            remote(slot, slot, fwd_send_sem.at[k], fwd_recv_sem.at[k], sibling).start()
        wait_bytes(full.at[pl.ds(0, NY * CROWS)], fwd_recv_sem.at[k])
        wait_bytes(full.at[pl.ds(0, NY * CROWS)], fwd_send_sem.at[k])
        wait_bytes(full.at[pl.ds(0, (NY - 1) * CROWS)], dir_send_sem.at[k])

    def scatter_dp(k):
        for i in range(NY):
            at = y_at(i)
            src = rows_at(grad_send.at[k], at * 2 + 1 - core, CROWS)
            remote(src, rows_at(pair_recv.at[k], at, CROWS), pair_send_sem.at[k], pair_recv_sem.at[k, at], sibling).start()
        slot = rows_at(grad_recv.at[k], y, CROWS)
        for i in range(NY):
            at = y_at(i)
            rows = pl.ds(pl.multiple_of(at * CROWS, CROWS), CROWS)
            wait_bytes(pair_recv.at[k, rows], pair_recv_sem.at[k, at])
            both = grad_send[k, pl.ds(pl.multiple_of((at * 2 + core) * CROWS, CROWS), CROWS), :] + pair_recv[k, rows, :]
            if i < NY - 1:
                grad_pair[k, rows, :] = both.astype(BF16)
                remote(
                    grad_pair.at[k, rows], slot, grad_send_sem.at[k], grad_recv_sem.at[k, y], (at * 2 + core, cell)
                ).start()
            else:
                total = both
        for i in range(NY - 1):
            src = y_at(NY - 2 - i)
            rows = pl.ds(pl.multiple_of(src * CROWS, CROWS), CROWS)
            wait_bytes(grad_recv.at[k, rows], grad_recv_sem.at[k, src])
            total = total + grad_recv[k, rows, :].astype(F32)
        wait_bytes(grad_recv.at[k, pl.ds(0, (NY - 1) * CROWS)], grad_send_sem.at[k])
        wait_bytes(pair_recv.at[k], pair_send_sem.at[k])
        return total

    def scatter_cells(k):
        for i in range(NZ):
            to = z_at(i)
            slot = rows_at(line_recv.at[k], to * NX + x, DROWS)
            for j in range(NX - 1):
                src = rows_at(image_send.at[k], to * NX + x_at(j), DROWS)
                remote(src, slot, line_send_sem.at[k], line_recv_sem.at[k, to], (dp, z * NX + x_at(j))).start()
        for i in range(NZ):
            to = z_at(i)
            wait_bytes(line_recv.at[k, pl.ds(0, (NX - 1) * DROWS)], line_recv_sem.at[k, to])
            total = image_exact[rows_of(to * NX + x, DROWS), :]
            for j in range(NX - 1):
                total = total + line_recv[k, rows_of(to * NX + x_at(j), DROWS), :].astype(F32)
            if i < NZ - 1:
                image_line[k, rows_of(to, DROWS), :] = total
                remote(
                    rows_at(image_line.at[k], to, DROWS),
                    rows_at(image_recv.at[k], z, DROWS),
                    image_send_sem.at[k],
                    image_recv_sem.at[k, z],
                    (dp, to * NX + x),
                ).start()
        for i in range(NZ - 1):
            src = z_at(NZ - 2 - i)
            wait_bytes(rows_at(image_recv.at[k], src, DROWS), image_recv_sem.at[k, src])
            total = total + image_recv[k, rows_of(src, DROWS), :]
        wait_bytes(line_recv.at[k, pl.ds(0, NZ * (NX - 1) * DROWS)], line_send_sem.at[k])
        wait_bytes(image_recv.at[k, pl.ds(0, (NZ - 1) * DROWS)], image_send_sem.at[k])
        return total

    def column(values):
        return jnp.sum(values, axis=0, keepdims=True)

    def size_of(values):
        most = jnp.max(jnp.abs(values), axis=0, keepdims=True)
        unit = values * (1.0 / jnp.maximum(most, TINY))
        return most * jnp.sqrt(column(unit * unit))

    def sum_start(k, rows):
        sums_mine[k] = jnp.zeros((8, COLS), F32)
        for i, row in enumerate(rows):
            sums_mine[k, pl.ds(i, 1), :] = row
        mine = sums_mine.at[k]
        over_dp(
            lambda p: remote(mine, sums_dp.at[k, dp], small_send_sem.at[k, 0], small_recv_sem.at[k, 0], (p, cell)).start()
        )
        sums_dp[k, dp] = sums_mine[k]

    def sum_middle(k, extra=None):
        wait_bytes(sums_dp.at[k, pl.ds(0, N_DP - 1)], small_recv_sem.at[k, 0])
        sums_mid[k] = jnp.sum(sums_dp[k], axis=0)
        if extra is not None:
            sums_mid[k, pl.ds(7, 1), :] = extra
        half = sums_mid.at[k]
        over_cells(
            lambda p: remote(
                half, sums_cell.at[k, cell], small_send_sem.at[k, 1], small_recv_sem.at[k, 1], (dp, p)
            ).start()
        )
        sums_cell[k, cell] = sums_mid[k]

    def sum_end(k, n):
        wait_bytes(sums_cell.at[k, pl.ds(0, N_CELL - 1)], small_recv_sem.at[k, 1])
        total = jnp.sum(sums_cell[k], axis=0)
        wait_bytes(sums_dp.at[k, pl.ds(0, N_DP - 1)], small_send_sem.at[k, 0])
        wait_bytes(sums_cell.at[k, pl.ds(0, N_CELL - 1)], small_send_sem.at[k, 1])
        return [total[i : i + 1] for i in range(n)]

    gather_cells(0)
    apply(tiles_t, row_of, col_of, residual_full.at[0], [grad_send.at[0]])
    gradient = scatter_dp(0)
    model_out[...] = gradient

    direction_full[0, my_cells, :] = gradient.astype(BF16)
    gather_dp(0)
    apply(tiles, col_of, row_of, direction_full.at[0], [image_send.at[0], image_exact])
    image = scatter_cells(0)
    residual_out[...] = image

    first = model_out[...]
    sum_start(0, [column(first * first), column(image * image)])
    observed_size = size_of(observed[...])
    scale = jnp.clip(observed_size / jnp.maximum(size_of(image), TINY), 1e-18, 1e18)
    scale = jnp.where(observed_size > 0.0, scale, 1.0)
    residual_full[1, my_rows, :] = (observed[...] - scale * image).astype(BF16)
    inverse = 1.0 / scale
    gather_cells(1, lambda: sum_middle(0, inverse))
    gamma, delta = sum_end(0, 2)
    alpha = gamma / delta

    for c in range(N_CELL):
        share = alpha * sums_cell[0, c, pl.ds(7, 1), :]
        for part in range(DROWS // 16):
            at = c * DROWS + part * 16
            old = residual_full[0, pl.ds(at, 16), :].astype(F32)
            new = residual_full[1, pl.ds(at, 16), :].astype(F32)
            value = old + share * (new - old)
            high = value.astype(BF16)
            into = pl.ds(at % BLOCK, 16)
            wide_pieces[at // BLOCK, into, pl.ds(0, COLS)] = high
            wide_pieces[at // BLOCK, into, pl.ds(COLS, COLS)] = (value - high.astype(F32)).astype(BF16)
    for slot in range(SLOTS):
        both = jnp.dot(tiles_t[slot], wide_pieces[row_of[0, 0, slot]], preferred_element_type=F32)
        prod[slot] = both[:, :COLS] + both[:, COLS:]
    place(col_of, [grad_send.at[1]])
    gradient = scatter_dp(1)

    direction_full[1, my_cells, :] = gradient.astype(BF16)
    gather_dp(1)
    apply(tiles, col_of, row_of, direction_full.at[1], [image_send.at[1], image_exact])
    update = scatter_cells(1)
    image = residual_out[...]
    sum_start(1, [column(gradient * gradient), column(update * update), column(update * image)])
    sum_middle(1)
    gamma_one, update_square, cross = sum_end(1, 3)
    beta = gamma_one / gamma
    delta_one = update_square + beta * (2.0 * cross + beta * delta)
    alpha_one = gamma_one / delta_one
    first = model_out[...]
    model_out[...] = alpha * first + alpha_one * (gradient + beta * first)
    residual_out[...] = observed[...] - alpha * image - alpha_one * (update + beta * image)


def shards(blocks, row_block, col_block, counts, observed):
    vmem = pl.BlockSpec(memory_space=pltpu.VMEM)
    smem = pl.BlockSpec(memory_space=pltpu.SMEM)
    dma = pltpu.SemaphoreType.DMA
    return pl.pallas_call(
        cgls,
        out_shape=(
            jax.ShapeDtypeStruct((CROWS, COLS), F32),
            jax.ShapeDtypeStruct((DROWS, COLS), F32),
        ),
        in_specs=[pl.BlockSpec(memory_space=pl.ANY), smem, smem, smem, vmem],
        out_specs=(vmem, vmem),
        scratch_shapes=[
            pltpu.VMEM((SLOTS, BLOCK, BLOCK), BF16),
            pltpu.VMEM((SLOTS, BLOCK, BLOCK), BF16),
            pltpu.VMEM((6, BLOCK, COLS), BF16),
            pltpu.VMEM((6, BLOCK, 2 * COLS), BF16),
            pltpu.VMEM((SLOTS, BLOCK, COLS), F32),
            pltpu.VMEM((TILE, COLS), F32),
            pltpu.VMEM((2, TILE, COLS), BF16),
            pltpu.VMEM((2, TILE, COLS), BF16),
            pltpu.VMEM((2, TILE, COLS), F32),
            pltpu.VMEM((2, TILE // 2, COLS), F32),
            pltpu.VMEM((2, TILE // 2, COLS), BF16),
            pltpu.VMEM((2, TILE // 2, COLS), BF16),
            pltpu.VMEM((2, TILE, COLS), BF16),
            pltpu.VMEM((2, TILE, COLS), BF16),
            pltpu.VMEM((2, NZ * DROWS, COLS), F32),
            pltpu.VMEM((2, NZ * DROWS, COLS), F32),
            pltpu.VMEM((2, 8, COLS), F32),
            pltpu.VMEM((2, N_DP, 8, COLS), F32),
            pltpu.VMEM((2, 8, COLS), F32),
            pltpu.VMEM((2, N_CELL, 8, COLS), F32),
            dma,
            dma((2,)),
            dma((2, NZ)),
            dma((2,)),
            dma((2,)),
            dma((2, NY)),
            dma((2,)),
            dma((2,)),
            dma((2,)),
            dma((2, NY)),
            dma((2,)),
            dma((2, NY)),
            dma((2,)),
            dma((2, NZ)),
            dma((2,)),
            dma((2, NZ)),
            dma((2, 2)),
            dma((2, 2)),
        ],
        compiler_params=pltpu.CompilerParams(
            collective_id=0, has_side_effects=True, vmem_limit_bytes=60 * 1024 * 1024
        ),
        name="cgls",
    )(blocks[0, 0], row_block, col_block, counts, observed)


def solution(mesh):
    in_specs = (
        P("dp", "cell", None, None, None),
        P("dp", "cell", None),
        P("dp", "cell", None),
        P("dp", "cell"),
        P(("dp", "cell"), None),
    )
    out_specs = (P(("cell", "dp"), None), P(("dp", "cell"), None))
    return jax.shard_map(shards, mesh=mesh, in_specs=in_specs, out_specs=out_specs, check_vma=False)
```

```python
import jax
import jax.numpy as jnp
from jax import lax
from jax.experimental import pallas as pl
from jax.experimental.pallas import tpu as pltpu
from jax.sharding import PartitionSpec as P

F32 = jnp.float32
BF16 = jnp.bfloat16
MESH = pl.DeviceIdType.MESH
SLOTS = 8
BLOCK = 256
NY = 8
NZ = 8
NX = 4
N_DP = NY * 2
N_CELL = NZ * NX
TILE = 6 * BLOCK
DROWS = TILE // N_CELL
CROWS = TILE // N_DP
HALF = CROWS // 2
COLS = 128
TINY = 1e-30


def far_first(i, n):
    return n // 2 - (i + 1) // 2 if i % 2 == 1 else (n // 2 + i // 2) % n


def rows_of(index, size):
    return pl.ds(pl.multiple_of(index * size, size), size)


def rows_at(ref, index, size):
    return ref.at[rows_of(index, size)]


def cgls(
    tiles_hbm,
    row_of,
    col_of,
    counts,
    observed,
    model_out,
    residual_out,
    tiles,
    tiles_t,
    pieces,
    wide_pieces,
    prod,
    image_exact,
    gradient,
    residual_full,
    direction_full,
    grad_send,
    pair_recv,
    grad_pair,
    grad_recv,
    image_send,
    line_recv,
    image_line,
    image_recv,
    sums_mine,
    sums_dp,
    sums_mid,
    sums_cell,
    load_sem,
    gather_send_sem,
    gather_z_sem,
    gather_x_sem,
    dir_send_sem,
    dir_recv_sem,
    fwd_send_sem,
    fwd_recv_sem,
    pair_send_sem,
    pair_recv_sem,
    grad_send_sem,
    grad_recv_sem,
    line_send_sem,
    line_recv_sem,
    image_send_sem,
    image_recv_sem,
    small_send_sem,
    small_recv_sem,
):
    dp = lax.axis_index("dp")
    cell = lax.axis_index("cell")
    y, core = dp // 2, dp % 2
    z, x = cell // NX, cell % NX
    sibling = (y * 2 + 1 - core, cell)
    my_rows = pl.ds(pl.multiple_of(cell * DROWS, DROWS), DROWS)

    load = pltpu.make_async_copy(tiles_hbm, tiles, load_sem)
    load.start()

    def z_at(i):
        return (z + far_first(i, NZ)) % NZ

    def x_at(i):
        return (x + far_first(i, NX)) % NX

    def y_at(i):
        return (y + far_first(i, NY)) % NY

    def over_cells(step):
        for i in range(N_CELL - 1):
            step(z_at(i // NX) * NX + x_at(i % NX))

    def over_dp(step):
        for i in range(N_DP - 1):
            step(y_at(i // 2) * 2 + (core + 1 + i) % 2)

    def remote(src, dst, send, recv, device):
        return pltpu.make_async_remote_copy(
            src_ref=src, dst_ref=dst, send_sem=send, recv_sem=recv, device_id=device, device_id_type=MESH
        )

    def wait_bytes(ref, sem):
        pltpu.make_async_copy(ref, ref, sem).wait()

    barrier = pltpu.get_barrier_semaphore()
    greet = [(dp, z_at(i) * NX + x) for i in range(NZ - 1)] + [(y_at(i) * 2 + core, cell) for i in range(NY - 1)]
    greet += [(dp, z * NX + x_at(i)) for i in range(NX - 1)] + [sibling]
    for device in greet:
        pl.semaphore_signal(barrier, inc=1, device_id=device, device_id_type=MESH)
    residual_full[0, my_rows, :] = observed[...].astype(BF16)
    load.wait()
    for slot in range(SLOTS):
        tiles_t[slot] = tiles[slot].T
    pl.semaphore_wait(barrier, len(greet))

    used = counts[0, 0]

    def multiply(matrix, source):
        for slot in range(SLOTS):
            prod[slot] = jnp.dot(matrix[slot], pieces[source[0, 0, slot]], preferred_element_type=F32)

    def apply(matrix, source, target, vector, sends):
        for at in range(6):
            pieces[at] = vector[pl.ds(at * BLOCK, BLOCK), :]
        multiply(matrix, source)
        place(target, sends)

    def place(target, sends):
        def one(at, carry):
            total = jnp.zeros((BLOCK, COLS), F32)
            for slot in range(SLOTS):
                here = jnp.logical_and(target[0, 0, slot] == at, slot < used)
                total = total + here.astype(F32) * prod[slot]
            for send in sends:
                send[rows_of(at, BLOCK), :] = total.astype(send.dtype)
            return carry

        lax.fori_loop(0, 6, one, 0)

    def gather_cells(k, between=None):
        full = residual_full.at[k]
        mine = full.at[my_rows]
        for i in range(NZ - 1):
            remote(mine, mine, gather_send_sem.at[k], gather_z_sem.at[k, z], (dp, z_at(i) * NX + x)).start()
        for i in range(NX - 1):
            remote(mine, mine, gather_send_sem.at[k], gather_x_sem.at[k], (dp, z * NX + x_at(i))).start()
        for i in range(NZ - 1):
            if i == 4 and between is not None:
                between()
            src = z_at(NZ - 2 - i)
            slot = rows_at(full, src * NX + x, DROWS)
            wait_bytes(slot, gather_z_sem.at[k, src])
            for j in range(NX - 1):
                remote(slot, slot, gather_send_sem.at[k], gather_x_sem.at[k], (dp, z * NX + x_at(j))).start()
        wait_bytes(full.at[pl.ds(0, NZ * (NX - 1) * DROWS)], gather_x_sem.at[k])

    def pass_dp(k):
        full = direction_full.at[k]

        def half(index, h):
            return pl.ds(pl.multiple_of(index * CROWS + h * HALF, HALF), HALF)

        for i in range(NY):
            at = y_at(i)
            src = rows_at(grad_send.at[k], at * 2 + 1 - core, CROWS)
            remote(src, rows_at(pair_recv.at[k], at, CROWS), pair_send_sem.at[k], pair_recv_sem.at[k, at], sibling).start()
        totals = []
        for h in range(2):
            for i in range(NY):
                at = y_at(i)
                if h == 0:
                    wait_bytes(rows_at(pair_recv.at[k], at, CROWS), pair_recv_sem.at[k, at])
                both = grad_send[k, half(at * 2 + core, h), :] + pair_recv[k, half(at, h), :]
                if i < NY - 1:
                    grad_pair[k, half(at, h), :] = both.astype(BF16)
                    remote(
                        grad_pair.at[k, half(at, h)],
                        grad_recv.at[k, half(y, h)],
                        grad_send_sem.at[k],
                        grad_recv_sem.at[k, h, y],
                        (at * 2 + core, cell),
                    ).start()
                else:
                    totals.append(both)
        for h in range(2):
            total = totals[h]
            for i in range(NY - 1):
                src = y_at(NY - 2 - i)
                wait_bytes(grad_recv.at[k, half(src, h)], grad_recv_sem.at[k, h, src])
                total = total + grad_recv[k, half(src, h), :].astype(F32)
            gradient[k, pl.ds(h * HALF, HALF), :] = total
            mine = full.at[half(dp, h)]
            direction_full[k, half(dp, h), :] = total.astype(BF16)
            for i in range(NY - 1):
                remote(mine, mine, dir_send_sem.at[k], dir_recv_sem.at[k, h, y], (y_at(i) * 2 + core, cell)).start()
            remote(mine, mine, fwd_send_sem.at[k], fwd_recv_sem.at[k], sibling).start()
        for h in range(2):
            for i in range(NY - 1):
                src = y_at(NY - 2 - i)
                slot = full.at[half(src * 2 + core, h)]
                wait_bytes(slot, dir_recv_sem.at[k, h, src])
                remote(slot, slot, fwd_send_sem.at[k], fwd_recv_sem.at[k], sibling).start()
        wait_bytes(full.at[pl.ds(0, NY * CROWS)], fwd_recv_sem.at[k])

    def scatter_cells(k):
        for i in range(NZ):
            to = z_at(i)
            slot = rows_at(line_recv.at[k], to * NX + x, DROWS)
            for j in range(NX - 1):
                src = rows_at(image_send.at[k], to * NX + x_at(j), DROWS)
                remote(src, slot, line_send_sem.at[k], line_recv_sem.at[k, to], (dp, z * NX + x_at(j))).start()
        for i in range(NZ):
            to = z_at(i)
            wait_bytes(line_recv.at[k, pl.ds(0, (NX - 1) * DROWS)], line_recv_sem.at[k, to])
            total = image_exact[rows_of(to * NX + x, DROWS), :]
            for j in range(NX - 1):
                total = total + line_recv[k, rows_of(to * NX + x_at(j), DROWS), :].astype(F32)
            if i < NZ - 1:
                image_line[k, rows_of(to, DROWS), :] = total
                remote(
                    rows_at(image_line.at[k], to, DROWS),
                    rows_at(image_recv.at[k], z, DROWS),
                    image_send_sem.at[k],
                    image_recv_sem.at[k, z],
                    (dp, to * NX + x),
                ).start()
        for i in range(NZ - 1):
            src = z_at(NZ - 2 - i)
            wait_bytes(rows_at(image_recv.at[k], src, DROWS), image_recv_sem.at[k, src])
            total = total + image_recv[k, rows_of(src, DROWS), :]
        return total

    def column(values):
        return jnp.sum(values, axis=0, keepdims=True)

    def size_of(values):
        most = jnp.max(jnp.abs(values), axis=0, keepdims=True)
        unit = values * (1.0 / jnp.maximum(most, TINY))
        return most * jnp.sqrt(column(unit * unit))

    def sum_start(k, rows):
        sums_mine[k] = jnp.zeros((8, COLS), F32)
        for i, row in enumerate(rows):
            sums_mine[k, pl.ds(i, 1), :] = row
        mine = sums_mine.at[k]
        over_dp(
            lambda p: remote(mine, sums_dp.at[k, dp], small_send_sem.at[k, 0], small_recv_sem.at[k, 0], (p, cell)).start()
        )
        sums_dp[k, dp] = sums_mine[k]

    def sum_middle(k, extra=None):
        wait_bytes(sums_dp.at[k, pl.ds(0, N_DP - 1)], small_recv_sem.at[k, 0])
        sums_mid[k] = jnp.sum(sums_dp[k], axis=0)
        if extra is not None:
            sums_mid[k, pl.ds(7, 1), :] = extra
        half = sums_mid.at[k]
        over_cells(
            lambda p: remote(
                half, sums_cell.at[k, cell], small_send_sem.at[k, 1], small_recv_sem.at[k, 1], (dp, p)
            ).start()
        )
        sums_cell[k, cell] = sums_mid[k]

    def sum_end(k, n):
        wait_bytes(sums_cell.at[k, pl.ds(0, N_CELL - 1)], small_recv_sem.at[k, 1])
        total = jnp.sum(sums_cell[k], axis=0)
        return [total[i : i + 1] for i in range(n)]

    def wait_sends(k):
        wait_bytes(residual_full.at[k, pl.ds(0, (N_CELL - 1) * DROWS)], gather_send_sem.at[k])
        wait_bytes(pair_recv.at[k], pair_send_sem.at[k])
        wait_bytes(grad_recv.at[k, pl.ds(0, (NY - 1) * CROWS)], grad_send_sem.at[k])
        wait_bytes(direction_full.at[k, pl.ds(0, (NY - 1) * CROWS)], dir_send_sem.at[k])
        wait_bytes(direction_full.at[k, pl.ds(0, NY * CROWS)], fwd_send_sem.at[k])
        wait_bytes(line_recv.at[k, pl.ds(0, NZ * (NX - 1) * DROWS)], line_send_sem.at[k])
        wait_bytes(image_recv.at[k, pl.ds(0, (NZ - 1) * DROWS)], image_send_sem.at[k])
        wait_bytes(sums_dp.at[k, pl.ds(0, N_DP - 1)], small_send_sem.at[k, 0])
        wait_bytes(sums_cell.at[k, pl.ds(0, N_CELL - 1)], small_send_sem.at[k, 1])

    gather_cells(0)
    apply(tiles_t, row_of, col_of, residual_full.at[0], [grad_send.at[0]])
    pass_dp(0)

    apply(tiles, col_of, row_of, direction_full.at[0], [image_send.at[0], image_exact])
    image = scatter_cells(0)
    residual_out[...] = image

    first = gradient[0]
    sum_start(0, [column(first * first), column(image * image)])
    observed_size = size_of(observed[...])
    scale = jnp.clip(observed_size / jnp.maximum(size_of(image), TINY), 1e-18, 1e18)
    scale = jnp.where(observed_size > 0.0, scale, 1.0)
    residual_full[1, my_rows, :] = (observed[...] - scale * image).astype(BF16)
    inverse = 1.0 / scale
    gather_cells(1, lambda: sum_middle(0, inverse))
    gamma, delta = sum_end(0, 2)
    alpha = gamma / delta

    for c in range(N_CELL):
        share = alpha * sums_cell[0, c, pl.ds(7, 1), :]
        for part in range(DROWS // 16):
            at = c * DROWS + part * 16
            old = residual_full[0, pl.ds(at, 16), :].astype(F32)
            new = residual_full[1, pl.ds(at, 16), :].astype(F32)
            value = old + share * (new - old)
            high = value.astype(BF16)
            into = pl.ds(at % BLOCK, 16)
            wide_pieces[at // BLOCK, into, pl.ds(0, COLS)] = high
            wide_pieces[at // BLOCK, into, pl.ds(COLS, COLS)] = (value - high.astype(F32)).astype(BF16)
    for slot in range(SLOTS):
        both = jnp.dot(tiles_t[slot], wide_pieces[row_of[0, 0, slot]], preferred_element_type=F32)
        prod[slot] = both[:, :COLS] + both[:, COLS:]
    place(col_of, [grad_send.at[1]])
    pass_dp(1)

    apply(tiles, col_of, row_of, direction_full.at[1], [image_send.at[1], image_exact])
    update = scatter_cells(1)
    image = residual_out[...]
    second = gradient[1]
    sum_start(1, [column(second * second), column(update * update), column(update * image)])
    sum_middle(1)
    gamma_one, update_square, cross = sum_end(1, 3)
    beta = gamma_one / gamma
    delta_one = update_square + beta * (2.0 * cross + beta * delta)
    alpha_one = gamma_one / delta_one
    first = gradient[0]
    model_out[...] = alpha * first + alpha_one * (gradient[1] + beta * first)
    residual_out[...] = observed[...] - alpha * image - alpha_one * (update + beta * image)
    wait_sends(0)
    wait_sends(1)


def shards(blocks, row_block, col_block, counts, observed):
    vmem = pl.BlockSpec(memory_space=pltpu.VMEM)
    smem = pl.BlockSpec(memory_space=pltpu.SMEM)
    dma = pltpu.SemaphoreType.DMA
    return pl.pallas_call(
        cgls,
        out_shape=(
            jax.ShapeDtypeStruct((CROWS, COLS), F32),
            jax.ShapeDtypeStruct((DROWS, COLS), F32),
        ),
        in_specs=[pl.BlockSpec(memory_space=pl.ANY), smem, smem, smem, vmem],
        out_specs=(vmem, vmem),
        scratch_shapes=[
            pltpu.VMEM((SLOTS, BLOCK, BLOCK), BF16),
            pltpu.VMEM((SLOTS, BLOCK, BLOCK), BF16),
            pltpu.VMEM((6, BLOCK, COLS), BF16),
            pltpu.VMEM((6, BLOCK, 2 * COLS), BF16),
            pltpu.VMEM((SLOTS, BLOCK, COLS), F32),
            pltpu.VMEM((TILE, COLS), F32),
            pltpu.VMEM((2, CROWS, COLS), F32),
            pltpu.VMEM((2, TILE, COLS), BF16),
            pltpu.VMEM((2, TILE, COLS), BF16),
            pltpu.VMEM((2, TILE, COLS), F32),
            pltpu.VMEM((2, TILE // 2, COLS), F32),
            pltpu.VMEM((2, TILE // 2, COLS), BF16),
            pltpu.VMEM((2, TILE // 2, COLS), BF16),
            pltpu.VMEM((2, TILE, COLS), BF16),
            pltpu.VMEM((2, TILE, COLS), BF16),
            pltpu.VMEM((2, NZ * DROWS, COLS), F32),
            pltpu.VMEM((2, NZ * DROWS, COLS), F32),
            pltpu.VMEM((2, 8, COLS), F32),
            pltpu.VMEM((2, N_DP, 8, COLS), F32),
            pltpu.VMEM((2, 8, COLS), F32),
            pltpu.VMEM((2, N_CELL, 8, COLS), F32),
            dma,
            dma((2,)),
            dma((2, NZ)),
            dma((2,)),
            dma((2,)),
            dma((2, 2, NY)),
            dma((2,)),
            dma((2,)),
            dma((2,)),
            dma((2, NY)),
            dma((2,)),
            dma((2, 2, NY)),
            dma((2,)),
            dma((2, NZ)),
            dma((2,)),
            dma((2, NZ)),
            dma((2, 2)),
            dma((2, 2)),
        ],
        compiler_params=pltpu.CompilerParams(
            collective_id=0, has_side_effects=True, vmem_limit_bytes=60 * 1024 * 1024
        ),
        name="cgls",
    )(blocks[0, 0], row_block, col_block, counts, observed)


def solution(mesh):
    in_specs = (
        P("dp", "cell", None, None, None),
        P("dp", "cell", None),
        P("dp", "cell", None),
        P("dp", "cell"),
        P(("dp", "cell"), None),
    )
    out_specs = (P(("cell", "dp"), None), P(("dp", "cell"), None))
    return jax.shard_map(shards, mesh=mesh, in_specs=in_specs, out_specs=out_specs, check_vma=False)
```

```python
import jax
import jax.numpy as jnp
from jax import lax
from jax.experimental import pallas as pl
from jax.experimental.pallas import tpu as pltpu
from jax.sharding import PartitionSpec as P

F32 = jnp.float32
BF16 = jnp.bfloat16
MESH = pl.DeviceIdType.MESH
SLOTS = 8
BLOCK = 256
NY = 8
NZ = 8
NX = 4
N_DP = NY * 2
N_CELL = NZ * NX
TILE = 6 * BLOCK
DROWS = TILE // N_CELL
CROWS = TILE // N_DP
HALF = CROWS // 2
COLS = 128
TINY = 1e-30


def far_first(i, n):
    return n // 2 - (i + 1) // 2 if i % 2 == 1 else (n // 2 + i // 2) % n


def rows_of(index, size):
    return pl.ds(pl.multiple_of(index * size, size), size)


def rows_at(ref, index, size):
    return ref.at[rows_of(index, size)]


def cgls(
    tiles_hbm,
    row_of,
    col_of,
    counts,
    observed,
    model_out,
    residual_out,
    tiles,
    tiles_t,
    pieces,
    wide_pieces,
    prod,
    image_exact,
    gradient,
    residual_full,
    direction_full,
    grad_send,
    pair_recv,
    grad_pair,
    grad_recv,
    image_send,
    line_recv,
    image_line,
    image_recv,
    sums_mine,
    sums_dp,
    sums_mid,
    sums_cell,
    pair_sum,
    inverse_mine,
    inverse,
    scalars,
    load_sem,
    scale_send_sem,
    scale_recv_sem,
    gather_send_sem,
    gather_z_sem,
    gather_x_sem,
    dir_send_sem,
    dir_recv_sem,
    fwd_send_sem,
    fwd_recv_sem,
    pair_send_sem,
    pair_recv_sem,
    grad_send_sem,
    grad_recv_sem,
    line_send_sem,
    line_recv_sem,
    image_send_sem,
    image_recv_sem,
    small_send_sem,
    small_recv_sem,
):
    dp = lax.axis_index("dp")
    cell = lax.axis_index("cell")
    y, core = dp // 2, dp % 2
    z, x = cell // NX, cell % NX
    sibling = (y * 2 + 1 - core, cell)
    my_rows = pl.ds(pl.multiple_of(cell * DROWS, DROWS), DROWS)

    load = pltpu.make_async_copy(tiles_hbm, tiles, load_sem)
    load.start()

    def z_at(i):
        return (z + far_first(i, NZ)) % NZ

    def x_at(i):
        return (x + far_first(i, NX)) % NX

    def y_at(i):
        return (y + far_first(i, NY)) % NY

    def over_cells(step):
        for i in range(N_CELL - 1):
            step(z_at(i // NX) * NX + x_at(i % NX))

    def over_dp(step):
        for i in range(N_DP - 1):
            step(y_at(i // 2) * 2 + (core + 1 + i) % 2)

    def remote(src, dst, send, recv, device):
        return pltpu.make_async_remote_copy(
            src_ref=src, dst_ref=dst, send_sem=send, recv_sem=recv, device_id=device, device_id_type=MESH
        )

    def wait_bytes(ref, sem):
        pltpu.make_async_copy(ref, ref, sem).wait()

    barrier = pltpu.get_barrier_semaphore()
    greet = [(dp, z_at(i) * NX + x) for i in range(NZ - 1)] + [(y_at(i) * 2 + core, cell) for i in range(NY - 1)]
    greet += [(dp, z * NX + x_at(i)) for i in range(NX - 1)] + [sibling]
    for device in greet:
        pl.semaphore_signal(barrier, inc=1, device_id=device, device_id_type=MESH)
    residual_full[0, my_rows, :] = observed[...].astype(BF16)
    load.wait()
    for slot in range(SLOTS):
        tiles_t[slot] = tiles[slot].T
    pl.semaphore_wait(barrier, len(greet))

    used = counts[0, 0]

    def multiply(matrix, source):
        for slot in range(SLOTS):
            prod[slot] = jnp.dot(matrix[slot], pieces[source[0, 0, slot]], preferred_element_type=F32)

    def apply(matrix, source, target, vector, sends):
        for at in range(6):
            pieces[at] = vector[pl.ds(at * BLOCK, BLOCK), :]
        multiply(matrix, source)
        place(target, sends)

    def place(target, sends):
        def one(at, carry):
            total = jnp.zeros((BLOCK, COLS), F32)
            for slot in range(SLOTS):
                here = jnp.logical_and(target[0, 0, slot] == at, slot < used)
                total = total + here.astype(F32) * prod[slot]
            for send in sends:
                send[rows_of(at, BLOCK), :] = total.astype(send.dtype)
            return carry

        lax.fori_loop(0, 6, one, 0)

    def gather_cells(k, between=None, beside=None):
        full = residual_full.at[k]
        mine = full.at[my_rows]
        for i in range(NZ - 1):
            remote(mine, mine, gather_send_sem.at[k], gather_z_sem.at[k, z], (dp, z_at(i) * NX + x)).start()
        for i in range(NX - 1):
            remote(mine, mine, gather_send_sem.at[k], gather_x_sem.at[k], (dp, z * NX + x_at(i))).start()
        if beside is not None:
            beside()
        for i in range(NZ - 1):
            if i == 4 and between is not None:
                between()
            src = z_at(NZ - 2 - i)
            slot = rows_at(full, src * NX + x, DROWS)
            wait_bytes(slot, gather_z_sem.at[k, src])
            for j in range(NX - 1):
                remote(slot, slot, gather_send_sem.at[k], gather_x_sem.at[k], (dp, z * NX + x_at(j))).start()
        wait_bytes(full.at[pl.ds(0, NZ * (NX - 1) * DROWS)], gather_x_sem.at[k])

    def pass_dp(k, factor=None):
        full = direction_full.at[k]

        def half(index, h):
            return pl.ds(pl.multiple_of(index * CROWS + h * HALF, HALF), HALF)

        for i in range(NY):
            at = y_at(i)
            src = rows_at(grad_send.at[k], at * 2 + 1 - core, CROWS)
            remote(src, rows_at(pair_recv.at[k], at, CROWS), pair_send_sem.at[k], pair_recv_sem.at[k, at], sibling).start()
        if factor is not None:
            share = factor()
        totals = []
        for h in range(2):
            for i in range(NY):
                at = y_at(i)
                if h == 0:
                    wait_bytes(rows_at(pair_recv.at[k], at, CROWS), pair_recv_sem.at[k, at])
                both = grad_send[k, half(at * 2 + core, h), :] + pair_recv[k, half(at, h), :]
                if factor is None:
                    pair_sum[half(at, h), :] = both
                else:
                    both = pair_sum[half(at, h), :] + share * both
                if i < NY - 1:
                    grad_pair[k, half(at, h), :] = both.astype(BF16)
                    remote(
                        grad_pair.at[k, half(at, h)],
                        grad_recv.at[k, half(y, h)],
                        grad_send_sem.at[k],
                        grad_recv_sem.at[k, h, y],
                        (at * 2 + core, cell),
                    ).start()
                else:
                    totals.append(both)
        for h in range(2):
            total = totals[h]
            for i in range(NY - 1):
                src = y_at(NY - 2 - i)
                wait_bytes(grad_recv.at[k, half(src, h)], grad_recv_sem.at[k, h, src])
                total = total + grad_recv[k, half(src, h), :].astype(F32)
            gradient[k, pl.ds(h * HALF, HALF), :] = total
            mine = full.at[half(dp, h)]
            direction_full[k, half(dp, h), :] = total.astype(BF16)
            for i in range(NY - 1):
                remote(mine, mine, dir_send_sem.at[k], dir_recv_sem.at[k, h, y], (y_at(i) * 2 + core, cell)).start()
            remote(mine, mine, fwd_send_sem.at[k], fwd_recv_sem.at[k], sibling).start()
        for h in range(2):
            for i in range(NY - 1):
                src = y_at(NY - 2 - i)
                slot = full.at[half(src * 2 + core, h)]
                wait_bytes(slot, dir_recv_sem.at[k, h, src])
                remote(slot, slot, fwd_send_sem.at[k], fwd_recv_sem.at[k], sibling).start()
        wait_bytes(full.at[pl.ds(0, NY * CROWS)], fwd_recv_sem.at[k])

    def scatter_cells(k):
        for i in range(NZ):
            to = z_at(i)
            slot = rows_at(line_recv.at[k], to * NX + x, DROWS)
            for j in range(NX - 1):
                src = rows_at(image_send.at[k], to * NX + x_at(j), DROWS)
                remote(src, slot, line_send_sem.at[k], line_recv_sem.at[k, to], (dp, z * NX + x_at(j))).start()
        for i in range(NZ):
            to = z_at(i)
            wait_bytes(line_recv.at[k, pl.ds(0, (NX - 1) * DROWS)], line_recv_sem.at[k, to])
            total = image_exact[rows_of(to * NX + x, DROWS), :]
            for j in range(NX - 1):
                total = total + line_recv[k, rows_of(to * NX + x_at(j), DROWS), :].astype(F32)
            if i < NZ - 1:
                image_line[k, rows_of(to, DROWS), :] = total
                remote(
                    rows_at(image_line.at[k], to, DROWS),
                    rows_at(image_recv.at[k], z, DROWS),
                    image_send_sem.at[k],
                    image_recv_sem.at[k, z],
                    (dp, to * NX + x),
                ).start()
        for i in range(NZ - 1):
            src = z_at(NZ - 2 - i)
            wait_bytes(rows_at(image_recv.at[k], src, DROWS), image_recv_sem.at[k, src])
            total = total + image_recv[k, rows_of(src, DROWS), :]
        return total

    def column(values):
        return jnp.sum(values, axis=0, keepdims=True)

    def size_of(values):
        most = jnp.max(jnp.abs(values), axis=0, keepdims=True)
        unit = values * (1.0 / jnp.maximum(most, TINY))
        return most * jnp.sqrt(column(unit * unit))

    def share_scale():
        over_cells(lambda p: remote(inverse_mine, inverse.at[cell], scale_send_sem, scale_recv_sem, (dp, p)).start())

    def sum_start(k, rows):
        for i, row in enumerate(rows):
            sums_mine[k, pl.ds(i + 1, 1), :] = row
        mine = sums_mine.at[k]
        over_dp(
            lambda p: remote(mine, sums_dp.at[k, dp], small_send_sem.at[k, 0], small_recv_sem.at[k, 0], (p, cell)).start()
        )
        sums_dp[k, dp] = sums_mine[k]

    def sum_middle(k):
        wait_bytes(sums_dp.at[k, pl.ds(0, N_DP - 1)], small_recv_sem.at[k, 0])
        sums_mid[k] = jnp.sum(sums_dp[k], axis=0)
        half = sums_mid.at[k]
        over_cells(
            lambda p: remote(
                half, sums_cell.at[k, cell], small_send_sem.at[k, 1], small_recv_sem.at[k, 1], (dp, p)
            ).start()
        )
        sums_cell[k, cell] = sums_mid[k]

    def sum_end(k, n):
        wait_bytes(sums_cell.at[k, pl.ds(0, N_CELL - 1)], small_recv_sem.at[k, 1])
        total = jnp.sum(sums_cell[k], axis=0)
        return [total[i : i + 1] for i in range(n)]

    def wait_sends(k):
        wait_bytes(residual_full.at[k, pl.ds(0, (N_CELL - 1) * DROWS)], gather_send_sem.at[k])
        wait_bytes(pair_recv.at[k], pair_send_sem.at[k])
        wait_bytes(grad_recv.at[k, pl.ds(0, (NY - 1) * CROWS)], grad_send_sem.at[k])
        wait_bytes(direction_full.at[k, pl.ds(0, (NY - 1) * CROWS)], dir_send_sem.at[k])
        wait_bytes(direction_full.at[k, pl.ds(0, NY * CROWS)], fwd_send_sem.at[k])
        wait_bytes(line_recv.at[k, pl.ds(0, NZ * (NX - 1) * DROWS)], line_send_sem.at[k])
        wait_bytes(image_recv.at[k, pl.ds(0, (NZ - 1) * DROWS)], image_send_sem.at[k])
        wait_bytes(sums_dp.at[k, pl.ds(0, N_DP - 1)], small_send_sem.at[k, 0])
        wait_bytes(sums_cell.at[k, pl.ds(0, N_CELL - 1)], small_send_sem.at[k, 1])

    gather_cells(0)
    apply(tiles_t, row_of, col_of, residual_full.at[0], [grad_send.at[0]])
    pass_dp(0)

    apply(tiles, col_of, row_of, direction_full.at[0], [image_send.at[0], image_exact])
    sums_mine[...] = jnp.zeros_like(sums_mine)
    sums_mine[0, pl.ds(0, 1), :] = column(gradient[0] * gradient[0])
    observed_size = size_of(observed[...])
    image = scatter_cells(0)
    sum_start(0, [column(image * image)])
    residual_out[...] = image

    scale = jnp.clip(observed_size / jnp.maximum(size_of(image), TINY), 1e-18, 1e18)
    scale = jnp.where(observed_size > 0.0, scale, 1.0)
    residual_full[1, my_rows, :] = (observed[...] - scale * image).astype(BF16)
    inverse_mine[...] = 1.0 / scale
    inverse[cell] = inverse_mine[...]
    gather_cells(1, lambda: sum_middle(0), share_scale)
    wait_bytes(inverse.at[pl.ds(0, N_CELL - 1)], scale_recv_sem)

    for c in range(N_CELL):
        factor = inverse[c]
        for part in range(DROWS // 16):
            at = c * DROWS + part * 16
            old = residual_full[0, pl.ds(at, 16), :].astype(F32)
            new = residual_full[1, pl.ds(at, 16), :].astype(F32)
            value = factor * (new - old)
            high = value.astype(BF16)
            into = pl.ds(at % BLOCK, 16)
            wide_pieces[at // BLOCK, into, pl.ds(0, COLS)] = high
            wide_pieces[at // BLOCK, into, pl.ds(COLS, COLS)] = (value - high.astype(F32)).astype(BF16)
    for slot in range(SLOTS):
        both = jnp.dot(tiles_t[slot], wide_pieces[row_of[0, 0, slot]], preferred_element_type=F32)
        prod[slot] = both[:, :COLS] + both[:, COLS:]
    place(col_of, [grad_send.at[1]])
    def alpha_now():
        gamma, delta = sum_end(0, 2)
        scalars[pl.ds(0, 1), :] = gamma
        scalars[pl.ds(1, 1), :] = delta
        return gamma / delta

    pass_dp(1, alpha_now)

    apply(tiles, col_of, row_of, direction_full.at[1], [image_send.at[1], image_exact])
    sums_mine[1, pl.ds(0, 1), :] = column(gradient[1] * gradient[1])
    update = scatter_cells(1)
    image = residual_out[...]
    sum_start(1, [column(update * update), column(update * image)])
    sum_middle(1)
    gamma_one, update_square, cross = sum_end(1, 3)
    gamma, delta = scalars[pl.ds(0, 1), :], scalars[pl.ds(1, 1), :]
    alpha = gamma / delta
    beta = gamma_one / gamma
    delta_one = update_square + beta * (2.0 * cross + beta * delta)
    alpha_one = gamma_one / delta_one
    first = gradient[0]
    model_out[...] = alpha * first + alpha_one * (gradient[1] + beta * first)
    residual_out[...] = observed[...] - alpha * image - alpha_one * (update + beta * image)
    wait_bytes(inverse.at[pl.ds(0, N_CELL - 1)], scale_send_sem)
    wait_sends(0)
    wait_sends(1)


def shards(blocks, row_block, col_block, counts, observed):
    vmem = pl.BlockSpec(memory_space=pltpu.VMEM)
    smem = pl.BlockSpec(memory_space=pltpu.SMEM)
    dma = pltpu.SemaphoreType.DMA
    return pl.pallas_call(
        cgls,
        out_shape=(
            jax.ShapeDtypeStruct((CROWS, COLS), F32),
            jax.ShapeDtypeStruct((DROWS, COLS), F32),
        ),
        in_specs=[pl.BlockSpec(memory_space=pl.ANY), smem, smem, smem, vmem],
        out_specs=(vmem, vmem),
        scratch_shapes=[
            pltpu.VMEM((SLOTS, BLOCK, BLOCK), BF16),
            pltpu.VMEM((SLOTS, BLOCK, BLOCK), BF16),
            pltpu.VMEM((6, BLOCK, COLS), BF16),
            pltpu.VMEM((6, BLOCK, 2 * COLS), BF16),
            pltpu.VMEM((SLOTS, BLOCK, COLS), F32),
            pltpu.VMEM((TILE, COLS), F32),
            pltpu.VMEM((2, CROWS, COLS), F32),
            pltpu.VMEM((2, TILE, COLS), BF16),
            pltpu.VMEM((2, TILE, COLS), BF16),
            pltpu.VMEM((2, TILE, COLS), F32),
            pltpu.VMEM((2, TILE // 2, COLS), F32),
            pltpu.VMEM((2, TILE // 2, COLS), BF16),
            pltpu.VMEM((2, TILE // 2, COLS), BF16),
            pltpu.VMEM((2, TILE, COLS), BF16),
            pltpu.VMEM((2, TILE, COLS), BF16),
            pltpu.VMEM((2, NZ * DROWS, COLS), F32),
            pltpu.VMEM((2, NZ * DROWS, COLS), F32),
            pltpu.VMEM((2, 4, COLS), F32),
            pltpu.VMEM((2, N_DP, 4, COLS), F32),
            pltpu.VMEM((2, 4, COLS), F32),
            pltpu.VMEM((2, N_CELL, 4, COLS), F32),
            pltpu.VMEM((TILE // 2, COLS), F32),
            pltpu.VMEM((1, COLS), F32),
            pltpu.VMEM((N_CELL, 1, COLS), F32),
            pltpu.VMEM((8, COLS), F32),
            dma,
            dma,
            dma,
            dma((2,)),
            dma((2, NZ)),
            dma((2,)),
            dma((2,)),
            dma((2, 2, NY)),
            dma((2,)),
            dma((2,)),
            dma((2,)),
            dma((2, NY)),
            dma((2,)),
            dma((2, 2, NY)),
            dma((2,)),
            dma((2, NZ)),
            dma((2,)),
            dma((2, NZ)),
            dma((2, 2)),
            dma((2, 2)),
        ],
        compiler_params=pltpu.CompilerParams(
            collective_id=0, has_side_effects=True, vmem_limit_bytes=60 * 1024 * 1024
        ),
        name="cgls",
    )(blocks[0, 0], row_block, col_block, counts, observed)


def solution(mesh):
    in_specs = (
        P("dp", "cell", None, None, None),
        P("dp", "cell", None),
        P("dp", "cell", None),
        P("dp", "cell"),
        P(("dp", "cell"), None),
    )
    out_specs = (P(("cell", "dp"), None), P(("dp", "cell"), None))
    return jax.shard_map(shards, mesh=mesh, in_specs=in_specs, out_specs=out_specs, check_vma=False)
```

```python
import jax
import jax.numpy as jnp
from jax import lax
from jax.experimental import pallas as pl
from jax.experimental.pallas import tpu as pltpu
from jax.sharding import PartitionSpec as P

F32 = jnp.float32
BF16 = jnp.bfloat16
MESH = pl.DeviceIdType.MESH
SLOTS = 8
BLOCK = 256
NY = 8
NZ = 8
NX = 4
N_DP = NY * 2
N_CELL = NZ * NX
TILE = 6 * BLOCK
DROWS = TILE // N_CELL
CROWS = TILE // N_DP
HALF = CROWS // 2
COLS = 128
TINY = 1e-30


def far_first(i, n):
    return n // 2 - (i + 1) // 2 if i % 2 == 1 else (n // 2 + i // 2) % n


def rows_of(index, size):
    return pl.ds(pl.multiple_of(index * size, size), size)


def rows_at(ref, index, size):
    return ref.at[rows_of(index, size)]


def cgls(
    tiles_hbm,
    row_of,
    col_of,
    counts,
    observed,
    model_out,
    residual_out,
    tiles,
    tiles_t,
    pieces,
    wide_pieces,
    prod,
    image_exact,
    gradient,
    residual_full,
    direction_full,
    grad_send,
    pair_recv,
    grad_pair,
    grad_recv,
    image_send,
    line_recv,
    image_line,
    image_recv,
    sums_mine,
    sums_dp,
    sums_mid,
    sums_cell,
    pair_sum,
    inverse_mine,
    inverse,
    scalars,
    load_sem,
    scale_send_sem,
    scale_recv_sem,
    gather_send_sem,
    gather_z_sem,
    gather_x_sem,
    dir_send_sem,
    dir_recv_sem,
    fwd_send_sem,
    fwd_recv_sem,
    pair_send_sem,
    pair_recv_sem,
    grad_send_sem,
    grad_recv_sem,
    line_send_sem,
    line_recv_sem,
    image_send_sem,
    image_recv_sem,
    small_send_sem,
    small_recv_sem,
):
    dp = lax.axis_index("dp")
    cell = lax.axis_index("cell")
    y, core = dp // 2, dp % 2
    z, x = cell // NX, cell % NX
    sibling = (y * 2 + 1 - core, cell)
    my_rows = pl.ds(pl.multiple_of(cell * DROWS, DROWS), DROWS)

    load = pltpu.make_async_copy(tiles_hbm, tiles, load_sem)
    load.start()

    def z_at(i):
        return (z + far_first(i, NZ)) % NZ

    def x_at(i):
        return (x + far_first(i, NX)) % NX

    def y_at(i):
        return (y + far_first(i, NY)) % NY

    def over_cells(step):
        for i in range(N_CELL - 1):
            step(z_at(i // NX) * NX + x_at(i % NX))

    def over_dp(step):
        for i in range(N_DP - 1):
            step(y_at(i // 2) * 2 + (core + 1 + i) % 2)

    def remote(src, dst, send, recv, device):
        return pltpu.make_async_remote_copy(
            src_ref=src, dst_ref=dst, send_sem=send, recv_sem=recv, device_id=device, device_id_type=MESH
        )

    def wait_bytes(ref, sem):
        pltpu.make_async_copy(ref, ref, sem).wait()

    barrier = pltpu.get_barrier_semaphore()
    greet = [(dp, z_at(i) * NX + x) for i in range(NZ - 1)] + [(y_at(i) * 2 + core, cell) for i in range(NY - 1)]
    greet += [(dp, z * NX + x_at(i)) for i in range(NX - 1)] + [sibling]
    for device in greet:
        pl.semaphore_signal(barrier, inc=1, device_id=device, device_id_type=MESH)
    residual_full[0, my_rows, :] = observed[...].astype(BF16)
    load.wait()
    for slot in range(SLOTS):
        tiles_t[slot] = tiles[slot].T
    pl.semaphore_wait(barrier, len(greet))

    used = counts[0, 0]

    def multiply(matrix, source):
        for slot in range(SLOTS):
            prod[slot] = jnp.dot(matrix[slot], pieces[source[0, 0, slot]], preferred_element_type=F32)

    def apply(matrix, source, target, vector, sends, after=None):
        for at in range(6):
            pieces[at] = vector[pl.ds(at * BLOCK, BLOCK), :]
        multiply(matrix, source)
        place(target, sends, after)

    def place(target, sends, after=None):
        for at in range(6):
            total = jnp.zeros((BLOCK, COLS), F32)
            for slot in range(SLOTS):
                here = jnp.logical_and(target[0, 0, slot] == at, slot < used)
                total = total + here.astype(F32) * prod[slot]
            for send in sends:
                send[pl.ds(at * BLOCK, BLOCK), :] = total.astype(send.dtype)
            if after is not None:
                after(at)

    def pair_copies(k):
        def after(at):
            for to in range(NY):
                if at * BLOCK < (to + 1) * 2 * CROWS <= (at + 1) * BLOCK:
                    remote(
                        rows_at(grad_send.at[k], to * 2 + 1 - core, CROWS),
                        pair_recv.at[k, pl.ds(to * CROWS, CROWS)],
                        pair_send_sem.at[k],
                        pair_recv_sem.at[k, to],
                        sibling,
                    ).start()

        return after

    def gather_cells(k, between=None, beside=None, arrived=None):
        full = residual_full.at[k]
        mine = full.at[my_rows]
        for i in range(NZ - 1):
            remote(mine, mine, gather_send_sem.at[k], gather_z_sem.at[k, z], (dp, z_at(i) * NX + x)).start()
        for i in range(NX - 1):
            remote(mine, mine, gather_send_sem.at[k], gather_x_sem.at[k, z], (dp, z * NX + x_at(i))).start()
        if beside is not None:
            beside()
        for i in range(NZ - 1):
            if i == 4 and between is not None:
                between()
            src = z_at(NZ - 2 - i)
            slot = rows_at(full, src * NX + x, DROWS)
            wait_bytes(slot, gather_z_sem.at[k, src])
            for j in range(NX - 1):
                remote(slot, slot, gather_send_sem.at[k], gather_x_sem.at[k, src], (dp, z * NX + x_at(j))).start()
        for i in range(NZ):
            src = z_at(NZ - 1 - i)
            wait_bytes(full.at[pl.ds(0, (NX - 1) * DROWS)], gather_x_sem.at[k, src])
            if arrived is not None:
                arrived(i, src)

    def pass_dp(k, factor=None):
        full = direction_full.at[k]

        def half(index, h):
            return pl.ds(pl.multiple_of(index * CROWS + h * HALF, HALF), HALF)

        if factor is not None:
            share = factor()
        totals = []
        for h in range(2):
            for i in range(NY):
                at = y_at(i)
                if h == 0:
                    wait_bytes(rows_at(pair_recv.at[k], at, CROWS), pair_recv_sem.at[k, at])
                both = grad_send[k, half(at * 2 + core, h), :] + pair_recv[k, half(at, h), :]
                if factor is None:
                    pair_sum[half(at, h), :] = both
                else:
                    both = pair_sum[half(at, h), :] + share * both
                if i < NY - 1:
                    grad_pair[k, half(at, h), :] = both.astype(BF16)
                    remote(
                        grad_pair.at[k, half(at, h)],
                        grad_recv.at[k, half(y, h)],
                        grad_send_sem.at[k],
                        grad_recv_sem.at[k, h, y],
                        (at * 2 + core, cell),
                    ).start()
                else:
                    totals.append(both)
        for h in range(2):
            total = totals[h]
            for i in range(NY - 1):
                src = y_at(NY - 2 - i)
                wait_bytes(grad_recv.at[k, half(src, h)], grad_recv_sem.at[k, h, src])
                total = total + grad_recv[k, half(src, h), :].astype(F32)
            gradient[k, pl.ds(h * HALF, HALF), :] = total
            mine = full.at[half(dp, h)]
            direction_full[k, half(dp, h), :] = total.astype(BF16)
            for i in range(NY - 1):
                remote(mine, mine, dir_send_sem.at[k], dir_recv_sem.at[k, h, y], (y_at(i) * 2 + core, cell)).start()
            remote(mine, mine, fwd_send_sem.at[k], fwd_recv_sem.at[k], sibling).start()
        for h in range(2):
            for i in range(NY - 1):
                src = y_at(NY - 2 - i)
                slot = full.at[half(src * 2 + core, h)]
                wait_bytes(slot, dir_recv_sem.at[k, h, src])
                remote(slot, slot, fwd_send_sem.at[k], fwd_recv_sem.at[k], sibling).start()
        wait_bytes(full.at[pl.ds(0, NY * CROWS)], fwd_recv_sem.at[k])

    def scatter_cells(k):
        for i in range(NZ):
            to = z_at(i)
            slot = rows_at(line_recv.at[k], to * NX + x, DROWS)
            for j in range(NX - 1):
                src = rows_at(image_send.at[k], to * NX + x_at(j), DROWS)
                remote(src, slot, line_send_sem.at[k], line_recv_sem.at[k, to], (dp, z * NX + x_at(j))).start()
        for i in range(NZ):
            to = z_at(i)
            wait_bytes(line_recv.at[k, pl.ds(0, (NX - 1) * DROWS)], line_recv_sem.at[k, to])
            total = image_exact[rows_of(to * NX + x, DROWS), :]
            for j in range(NX - 1):
                total = total + line_recv[k, rows_of(to * NX + x_at(j), DROWS), :].astype(F32)
            if i < NZ - 1:
                image_line[k, rows_of(to, DROWS), :] = total
                remote(
                    rows_at(image_line.at[k], to, DROWS),
                    rows_at(image_recv.at[k], z, DROWS),
                    image_send_sem.at[k],
                    image_recv_sem.at[k, z],
                    (dp, to * NX + x),
                ).start()
        for i in range(NZ - 1):
            src = z_at(NZ - 2 - i)
            wait_bytes(rows_at(image_recv.at[k], src, DROWS), image_recv_sem.at[k, src])
            total = total + image_recv[k, rows_of(src, DROWS), :]
        return total

    def column(values):
        return jnp.sum(values, axis=0, keepdims=True)

    def size_of(values):
        most = jnp.max(jnp.abs(values), axis=0, keepdims=True)
        unit = values * (1.0 / jnp.maximum(most, TINY))
        return most * jnp.sqrt(column(unit * unit))

    def share_scale():
        over_cells(lambda p: remote(inverse_mine, inverse.at[cell], scale_send_sem, scale_recv_sem, (dp, p)).start())

    def sum_start(k, rows):
        for i, row in enumerate(rows):
            sums_mine[k, pl.ds(i + 1, 1), :] = row
        mine = sums_mine.at[k]
        over_dp(
            lambda p: remote(mine, sums_dp.at[k, dp], small_send_sem.at[k, 0], small_recv_sem.at[k, 0], (p, cell)).start()
        )
        sums_dp[k, dp] = sums_mine[k]

    def sum_middle(k):
        wait_bytes(sums_dp.at[k, pl.ds(0, N_DP - 1)], small_recv_sem.at[k, 0])
        sums_mid[k] = jnp.sum(sums_dp[k], axis=0)
        half = sums_mid.at[k]
        over_cells(
            lambda p: remote(
                half, sums_cell.at[k, cell], small_send_sem.at[k, 1], small_recv_sem.at[k, 1], (dp, p)
            ).start()
        )
        sums_cell[k, cell] = sums_mid[k]

    def sum_end(k, n):
        wait_bytes(sums_cell.at[k, pl.ds(0, N_CELL - 1)], small_recv_sem.at[k, 1])
        total = jnp.sum(sums_cell[k], axis=0)
        return [total[i : i + 1] for i in range(n)]

    def wait_sends(k):
        wait_bytes(residual_full.at[k, pl.ds(0, (N_CELL - 1) * DROWS)], gather_send_sem.at[k])
        wait_bytes(pair_recv.at[k], pair_send_sem.at[k])
        wait_bytes(grad_recv.at[k, pl.ds(0, (NY - 1) * CROWS)], grad_send_sem.at[k])
        wait_bytes(direction_full.at[k, pl.ds(0, (NY - 1) * CROWS)], dir_send_sem.at[k])
        wait_bytes(direction_full.at[k, pl.ds(0, NY * CROWS)], fwd_send_sem.at[k])
        wait_bytes(line_recv.at[k, pl.ds(0, NZ * (NX - 1) * DROWS)], line_send_sem.at[k])
        wait_bytes(image_recv.at[k, pl.ds(0, (NZ - 1) * DROWS)], image_send_sem.at[k])
        wait_bytes(sums_dp.at[k, pl.ds(0, N_DP - 1)], small_send_sem.at[k, 0])
        wait_bytes(sums_cell.at[k, pl.ds(0, N_CELL - 1)], small_send_sem.at[k, 1])

    gather_cells(0)
    apply(tiles_t, row_of, col_of, residual_full.at[0], [grad_send.at[0]], pair_copies(0))
    pass_dp(0)

    apply(tiles, col_of, row_of, direction_full.at[0], [image_send.at[0], image_exact])
    sums_mine[...] = jnp.zeros_like(sums_mine)
    sums_mine[0, pl.ds(0, 1), :] = column(gradient[0] * gradient[0])
    observed_size = size_of(observed[...])
    image = scatter_cells(0)
    sum_start(0, [column(image * image)])
    residual_out[...] = image

    scale = jnp.clip(observed_size / jnp.maximum(size_of(image), TINY), 1e-18, 1e18)
    scale = jnp.where(observed_size > 0.0, scale, 1.0)
    residual_full[1, my_rows, :] = (observed[...] - scale * image).astype(BF16)
    inverse_mine[...] = 1.0 / scale
    inverse[cell] = inverse_mine[...]

    def change(i, src):
        if i == 0:
            wait_bytes(inverse.at[pl.ds(0, N_CELL - 1)], scale_recv_sem)
        for j in range(NX):
            c = src * NX + j
            factor = inverse[c]
            for part in range(DROWS // 16):
                at = c * DROWS + part * 16
                rows = pl.ds(pl.multiple_of(at, 16), 16)
                old = residual_full[0, rows, :].astype(F32)
                new = residual_full[1, rows, :].astype(F32)
                value = factor * (new - old)
                high = value.astype(BF16)
                into = pl.ds(pl.multiple_of(at % BLOCK, 16), 16)
                wide_pieces[at // BLOCK, into, pl.ds(0, COLS)] = high
                wide_pieces[at // BLOCK, into, pl.ds(COLS, COLS)] = (value - high.astype(F32)).astype(BF16)

    gather_cells(1, lambda: sum_middle(0), share_scale, change)
    for slot in range(SLOTS):
        both = jnp.dot(tiles_t[slot], wide_pieces[row_of[0, 0, slot]], preferred_element_type=F32)
        prod[slot] = both[:, :COLS] + both[:, COLS:]
    place(col_of, [grad_send.at[1]], pair_copies(1))
    def alpha_now():
        gamma, delta = sum_end(0, 2)
        scalars[pl.ds(0, 1), :] = gamma
        scalars[pl.ds(1, 1), :] = delta
        return gamma / delta

    pass_dp(1, alpha_now)

    apply(tiles, col_of, row_of, direction_full.at[1], [image_send.at[1], image_exact])
    sums_mine[1, pl.ds(0, 1), :] = column(gradient[1] * gradient[1])
    update = scatter_cells(1)
    image = residual_out[...]
    sum_start(1, [column(update * update), column(update * image)])
    sum_middle(1)
    gamma_one, update_square, cross = sum_end(1, 3)
    gamma, delta = scalars[pl.ds(0, 1), :], scalars[pl.ds(1, 1), :]
    alpha = gamma / delta
    beta = gamma_one / gamma
    delta_one = update_square + beta * (2.0 * cross + beta * delta)
    alpha_one = gamma_one / delta_one
    first = gradient[0]
    model_out[...] = alpha * first + alpha_one * (gradient[1] + beta * first)
    residual_out[...] = observed[...] - alpha * image - alpha_one * (update + beta * image)
    wait_bytes(inverse.at[pl.ds(0, N_CELL - 1)], scale_send_sem)
    wait_sends(0)
    wait_sends(1)


def shards(blocks, row_block, col_block, counts, observed):
    vmem = pl.BlockSpec(memory_space=pltpu.VMEM)
    smem = pl.BlockSpec(memory_space=pltpu.SMEM)
    dma = pltpu.SemaphoreType.DMA
    return pl.pallas_call(
        cgls,
        out_shape=(
            jax.ShapeDtypeStruct((CROWS, COLS), F32),
            jax.ShapeDtypeStruct((DROWS, COLS), F32),
        ),
        in_specs=[pl.BlockSpec(memory_space=pl.ANY), smem, smem, smem, vmem],
        out_specs=(vmem, vmem),
        scratch_shapes=[
            pltpu.VMEM((SLOTS, BLOCK, BLOCK), BF16),
            pltpu.VMEM((SLOTS, BLOCK, BLOCK), BF16),
            pltpu.VMEM((6, BLOCK, COLS), BF16),
            pltpu.VMEM((6, BLOCK, 2 * COLS), BF16),
            pltpu.VMEM((SLOTS, BLOCK, COLS), F32),
            pltpu.VMEM((TILE, COLS), F32),
            pltpu.VMEM((2, CROWS, COLS), F32),
            pltpu.VMEM((2, TILE, COLS), BF16),
            pltpu.VMEM((2, TILE, COLS), BF16),
            pltpu.VMEM((2, TILE, COLS), F32),
            pltpu.VMEM((2, TILE // 2, COLS), F32),
            pltpu.VMEM((2, TILE // 2, COLS), BF16),
            pltpu.VMEM((2, TILE // 2, COLS), BF16),
            pltpu.VMEM((2, TILE, COLS), BF16),
            pltpu.VMEM((2, TILE, COLS), BF16),
            pltpu.VMEM((2, NZ * DROWS, COLS), F32),
            pltpu.VMEM((2, NZ * DROWS, COLS), F32),
            pltpu.VMEM((2, 4, COLS), F32),
            pltpu.VMEM((2, N_DP, 4, COLS), F32),
            pltpu.VMEM((2, 4, COLS), F32),
            pltpu.VMEM((2, N_CELL, 4, COLS), F32),
            pltpu.VMEM((TILE // 2, COLS), F32),
            pltpu.VMEM((1, COLS), F32),
            pltpu.VMEM((N_CELL, 1, COLS), F32),
            pltpu.VMEM((8, COLS), F32),
            dma,
            dma,
            dma,
            dma((2,)),
            dma((2, NZ)),
            dma((2, NZ)),
            dma((2,)),
            dma((2, 2, NY)),
            dma((2,)),
            dma((2,)),
            dma((2,)),
            dma((2, NY)),
            dma((2,)),
            dma((2, 2, NY)),
            dma((2,)),
            dma((2, NZ)),
            dma((2,)),
            dma((2, NZ)),
            dma((2, 2)),
            dma((2, 2)),
        ],
        compiler_params=pltpu.CompilerParams(
            collective_id=0, has_side_effects=True, vmem_limit_bytes=56_200_000
        ),
        name="cgls",
    )(blocks[0, 0], row_block, col_block, counts, observed)


def solution(mesh):
    in_specs = (
        P("dp", "cell", None, None, None),
        P("dp", "cell", None),
        P("dp", "cell", None),
        P("dp", "cell"),
        P(("dp", "cell"), None),
    )
    out_specs = (P(("cell", "dp"), None), P(("dp", "cell"), None))
    return jax.shard_map(shards, mesh=mesh, in_specs=in_specs, out_specs=out_specs, check_vma=False)
```
